128 devices in a mesh: seq: 8 (over y, core), chan: 16 (over x, z).
Axes of the slice: x: 4, y: 4, z: 4, core: 2. Of those that a mesh axis runs over, the one named last changes fastest.
Arguments:
- query_proj: bfloat16 [16384, 4096], P(('seq', 'chan')), may hold values from -6 to 6
- key_proj: bfloat16 [16384, 4096], P(('seq', 'chan')), may hold values from -6 to 6
- value_proj: bfloat16 [16384, 4096], P(('seq', 'chan')), may hold values from -6 to 6
- filter_taps: bfloat16 [16384, 4096], P(('seq', 'chan')), may hold values from -0.046875 to 0.046875
- skip_gain: float32 [4096], replicated, may hold values from 0.5 to 1.5
Outputs:
- mixed: bfloat16 [16384, 4096], P(('seq', 'chan'))
The draws below stay inside these ranges and needn't reach their ends.
All inputs are finite; a program needn't handle non-finite values.
Results may differ from the reference program's by a relative error of at most 0.012.
Values may be sent and summed in bfloat16 or wider, within the bound.
A program may use at most 256 MiB of HBM per device.

```python
import math
import jax
import jax.numpy as jnp
from jax import lax

C = 4096
SEQ_LEN = 16384


def steps_of(rng, shape, pieces, low, top_value):
    loudness, own = 1.0, jax.random.fold_in(rng, 6)
    for axis_at, shards_of in pieces:
        draws = jnp.exp(jax.random.uniform(jax.random.fold_in(own, axis_at), (shards_of,), jnp.float32, low / len(pieces), top_value / len(pieces)))
        loudness = loudness * jnp.repeat(draws, shape[axis_at] // shards_of).reshape([-1 if axis == axis_at else 1 for axis in range(len(shape))])
    return loudness


def bell_draw(own_key, shape, spread, bound, pieces=(), dtype=jnp.bfloat16):
    array = spread * jax.random.normal(own_key, shape, jnp.float32)
    if pieces:
        array = array * steps_of(own_key, shape, pieces, -0.22, 0.18)
    return jnp.clip(array, -bound, bound).astype(dtype)


def setup_inputs(seed: int = 0) -> dict:
    streams_of = jax.random.split(jax.random.key(seed), 6)
    query_proj = bell_draw(streams_of[0], (SEQ_LEN, C), 1.0, 6.0, ((0, 128),))
    key_proj = bell_draw(streams_of[1], (SEQ_LEN, C), 1.0, 6.0, ((0, 128),))
    value_proj = bell_draw(streams_of[2], (SEQ_LEN, C), 1.0, 6.0, ((0, 128),))
    filter_taps = bell_draw(streams_of[3], (SEQ_LEN, C), SEQ_LEN ** -0.5, 0.046875, ((0, 128),))
    skip_gain = jnp.clip(jax.random.uniform(streams_of[4], (C,), jnp.float32, 0.5, 1.5), 0.5, 1.5)
    return {"query_proj": query_proj, "key_proj": key_proj, "value_proj": value_proj, "filter_taps": filter_taps, "skip_gain": skip_gain}


def reference(query_proj, key_proj, value_proj, filter_taps, skip_gain):
    product = (key_proj.astype(jnp.float32) * value_proj.astype(jnp.float32)).astype(jnp.bfloat16)
    signal = product.astype(jnp.float32)
    tap_values = filter_taps.astype(jnp.float32)
    padded = 2 * SEQ_LEN
    width_block = math.gcd(C, 256)
    blocks = C // width_block

    def convolve(members):
        sig_block, tap_block = members
        spectrum = jnp.fft.rfft(sig_block, n=padded, axis=0) * jnp.fft.rfft(tap_block, n=padded, axis=0)
        return jnp.fft.irfft(spectrum, n=padded, axis=0)[:SEQ_LEN]

    stacked = (signal.reshape(SEQ_LEN, blocks, width_block).transpose(1, 0, 2),
               tap_values.reshape(SEQ_LEN, blocks, width_block).transpose(1, 0, 2))
    convolved = lax.map(convolve, stacked).transpose(1, 0, 2).reshape(SEQ_LEN, C)
    mixed = query_proj.astype(jnp.float32) * (convolved + skip_gain * signal)
    return mixed.astype(jnp.bfloat16)
```

```python
import functools
import math

import jax
import jax.numpy as jnp
import numpy as np
from jax import lax
from jax.experimental import pallas as pl
from jax.experimental.pallas import tpu as pltpu
from jax.sharding import PartitionSpec as P

MESH = pl.DeviceIdType.MESH
DEVS = 128
TOK = 128
CHUNKS = 2
CC = 16
BLOCKS = 16
F32 = jnp.float32
BF16 = jnp.bfloat16


def tables():
    idx = np.arange(128)
    coarse = 2.0 * math.pi * np.outer(idx + 0.5, idx) / 256.0
    twist = 2.0 * math.pi * np.outer(idx + 0.5, idx) / 32768.0
    inner = 2.0 * math.pi * (np.outer(idx, idx) % 128) / 128.0
    fwd_outer = np.concatenate([np.cos(coarse), -np.sin(coarse)], axis=0)
    cos_in, sin_in = np.cos(inner), np.sin(inner)
    fwd_inner = np.block([[cos_in, -sin_in], [sin_in, cos_in]])
    inv_inner = np.block([[cos_in, sin_in], [-sin_in, cos_in]])
    inv_outer = np.concatenate([np.cos(coarse.T), -np.sin(coarse.T)], axis=1) * (2.0 / 32768.0)
    twists = np.stack([np.cos(twist), -np.sin(twist)])
    return (
        fwd_outer.astype(jnp.bfloat16),
        fwd_inner.astype(jnp.bfloat16),
        inv_inner.astype(jnp.bfloat16),
        inv_outer.astype(jnp.bfloat16),
        twists.astype(np.float32),
    )


def group_device(group):
    x = (group // 64) * 2 + (group // 4) % 2
    y = ((group // 32) % 2) * 2 + (group // 2) % 2
    z = ((group // 16) % 2) * 2 + group % 2
    core = (group // 8) % 2
    return y * 2 + core, x * 4 + z


def own_group(seq, chan):
    x, z = chan // 4, chan % 4
    y, core = seq // 2, seq % 2
    return (x // 2) * 64 + (y // 2) * 32 + (z // 2) * 16 + core * 8 + (x % 2) * 4 + (y % 2) * 2 + z % 2


def kernel(
    q_hbm, k_hbm, v_hbm, h_hbm, gain_hbm, fo_hbm, fi_hbm, ii_hbm, io_hbm, tw_hbm, out_hbm,
    q_buf, k_buf, v_buf, h_buf, gain_buf, fo_buf, fi_buf, ii_buf, io_buf, tw_buf, out_buf,
    send, recv, wide, ywide, ysend, yrecv,
    in_sem, out_sem, send_sem, recv_sem, own_sem, ysend_sem, yrecv_sem, yown_sem,
):
    seq, chan = lax.axis_index("seq"), lax.axis_index("chan")
    me = seq * 16 + chan
    group_me = own_group(seq, chan)

    pairs = (
        (k_hbm, k_buf), (v_hbm, v_buf), (h_hbm, h_buf), (fo_hbm, fo_buf), (fi_hbm, fi_buf), (ii_hbm, ii_buf),
        (io_hbm, io_buf), (tw_hbm, tw_buf), (q_hbm, q_buf), (gain_hbm, gain_buf),
    )
    loads = [pltpu.make_async_copy(src, dst, in_sem.at[i]) for i, (src, dst) in enumerate(pairs)]
    for load in loads:
        load.start()

    barrier = pltpu.get_barrier_semaphore()

    def greet(step, carry):
        peer = (me + step) % DEVS
        pl.semaphore_signal(barrier, inc=1, device_id=(peer // 16, peer % 16), device_id_type=MESH)
        return carry

    lax.fori_loop(1, DEVS, greet, 0)
    for load in loads[:3]:
        load.wait()
    pl.semaphore_wait(barrier, DEVS - 1)

    def pack(chunk, step, carry):
        block = (group_me // 8 + step) % BLOCKS
        lanes = pl.ds(pl.multiple_of(chunk * (BLOCKS * 128) + block * 128, 128), 128)
        product = (k_buf[:, lanes].astype(F32) * v_buf[:, lanes].astype(F32)).astype(BF16)
        send[chunk, pl.ds(block * 8, 8), 0] = product.T.reshape(8, CC, TOK)
        send[chunk, pl.ds(block * 8, 8), 1] = h_buf[:, lanes].T.reshape(8, CC, TOK)
        for near in range(8):
            group = block * 8 + (group_me + near) % 8
            seq_to, chan_to = group_device(group)

            @pl.when(group != group_me)
            def _():
                pltpu.make_async_remote_copy(
                    src_ref=send.at[chunk, group], dst_ref=recv.at[chunk, me],
                    send_sem=send_sem.at[chunk], recv_sem=recv_sem.at[chunk],
                    device_id=(seq_to, chan_to), device_id_type=MESH,
                ).start()

            @pl.when(group == group_me)
            def _():
                pltpu.make_async_copy(send.at[chunk, group], recv.at[chunk, me], own_sem.at[chunk]).start()

        return carry

    for chunk in range(CHUNKS):
        lax.fori_loop(0, BLOCKS, functools.partial(pack, chunk), 0)

    for load in loads[3:]:
        load.wait()

    others = pl.ds(0, DEVS - 1)

    def widen(chunk, step, carry):
        part = pl.ds(step * 8, 8)
        rows = pl.ds(pl.multiple_of(step * (8 * 2 * CC), 8 * 2 * CC), 8 * 2 * CC)
        wide[rows, :] = recv[chunk, part].reshape(8 * 2 * CC, TOK).astype(F32)
        return carry

    def transform(at, carry):
        twist_re, twist_im = tw_buf[0], tw_buf[1]
        turned = []
        for c in (2 * at, 2 * at + 1):
            x = wide[pl.ds(c, DEVS, 2 * CC), :].astype(BF16)
            h = wide[pl.ds(CC + c, DEVS, 2 * CC), :].astype(BF16)
            both = jnp.dot(fo_buf[...], jnp.concatenate([x, h], axis=1), preferred_element_type=F32)
            rows = []
            for lane in (0, 128):
                re, im = both[:128, lane:lane + 128], both[128:, lane:lane + 128]
                rows.append(jnp.concatenate(
                    [(re * twist_re - im * twist_im).astype(BF16), (re * twist_im + im * twist_re).astype(BF16)], axis=1))
            spectra = jnp.dot(jnp.concatenate(rows, axis=0), fi_buf[...], preferred_element_type=F32)
            x_re, x_im = spectra[:128, :128], spectra[:128, 128:]
            h_re, h_im = spectra[128:, :128], spectra[128:, 128:]
            mixed = jnp.concatenate(
                [(x_re * h_re - x_im * h_im).astype(BF16), (x_re * h_im + x_im * h_re).astype(BF16)], axis=1)
            back = jnp.dot(mixed, ii_buf[...], preferred_element_type=F32)
            re, im = back[:, :128], back[:, 128:]
            turned.append(jnp.concatenate(
                [(re * twist_re + im * twist_im).astype(BF16), (im * twist_re - re * twist_im).astype(BF16)], axis=0))
        y = jnp.dot(io_buf[...], jnp.concatenate(turned, axis=1), preferred_element_type=F32)
        ywide[pl.ds(2 * at, DEVS, CC), :] = y[:, :128]
        ywide[pl.ds(2 * at + 1, DEVS, CC), :] = y[:, 128:]
        return carry

    def give_back(chunk, step, carry):
        peer = (me + step) % DEVS
        ysend[chunk, peer] = ywide[pl.ds(pl.multiple_of(peer * CC, CC), CC), :].astype(BF16)

        @pl.when(step != 0)
        def _():
            pltpu.make_async_remote_copy(
                src_ref=ysend.at[chunk, peer], dst_ref=yrecv.at[chunk, group_me],
                send_sem=ysend_sem.at[chunk], recv_sem=yrecv_sem.at[chunk],
                device_id=(peer // 16, peer % 16), device_id_type=MESH,
            ).start()

        @pl.when(step == 0)
        def _():
            pltpu.make_async_copy(ysend.at[chunk, peer], yrecv.at[chunk, group_me], yown_sem.at[chunk]).start()

        return carry

    for chunk in range(CHUNKS):
        arrived = recv.at[chunk, others]
        pltpu.make_async_copy(arrived, arrived, recv_sem.at[chunk]).wait()
        pltpu.make_async_copy(recv.at[chunk, 0], recv.at[chunk, 0], own_sem.at[chunk]).wait()
        lax.fori_loop(0, 16, functools.partial(widen, chunk), 0)
        lax.fori_loop(0, CC // 2, transform, 0)
        lax.fori_loop(0, DEVS, functools.partial(give_back, chunk), 0)

    def gate(chunk, block, carry):
        lanes = pl.ds(pl.multiple_of(chunk * (BLOCKS * 128) + block * 128, 128), 128)
        convolved = yrecv[chunk, pl.ds(block * 8, 8)].reshape(128, TOK).T.astype(F32)
        product = (k_buf[:, lanes].astype(F32) * v_buf[:, lanes].astype(F32)).astype(BF16).astype(F32)
        out_buf[:, lanes] = (q_buf[:, lanes].astype(F32) * (convolved + gain_buf[:, lanes] * product)).astype(BF16)
        return carry

    stores = []
    for chunk in range(CHUNKS):
        arrived = yrecv.at[chunk, others]
        pltpu.make_async_copy(arrived, arrived, yrecv_sem.at[chunk]).wait()
        pltpu.make_async_copy(yrecv.at[chunk, 0], yrecv.at[chunk, 0], yown_sem.at[chunk]).wait()
        lax.fori_loop(0, BLOCKS, functools.partial(gate, chunk), 0)
        half = pl.ds(chunk * BLOCKS * 128, BLOCKS * 128)
        stores.append(pltpu.make_async_copy(out_buf.at[:, half], out_hbm.at[:, half], out_sem.at[chunk]))
        stores[-1].start()
    for store in stores:
        store.wait()
    for chunk in range(CHUNKS):
        left = send.at[chunk, others]
        pltpu.make_async_copy(left, left, send_sem.at[chunk]).wait()
        left = ysend.at[chunk, others]
        pltpu.make_async_copy(left, left, ysend_sem.at[chunk]).wait()


def shards(query_proj, key_proj, value_proj, filter_taps, skip_gain):
    whole = (TOK, 4096)
    any_spec = pl.BlockSpec(memory_space=pltpu.HBM)
    return pl.pallas_call(
        kernel,
        out_shape=jax.ShapeDtypeStruct(whole, BF16),
        in_specs=[any_spec] * 10,
        out_specs=any_spec,
        scratch_shapes=[
            pltpu.VMEM(whole, BF16), pltpu.VMEM(whole, BF16), pltpu.VMEM(whole, BF16), pltpu.VMEM(whole, BF16),
            pltpu.VMEM((1, 4096), F32),
            pltpu.VMEM((256, 128), BF16), pltpu.VMEM((256, 256), BF16), pltpu.VMEM((256, 256), BF16),
            pltpu.VMEM((128, 256), BF16), pltpu.VMEM((2, 128, 128), F32),
            pltpu.VMEM(whole, BF16),
            pltpu.VMEM((CHUNKS, DEVS, 2, CC, TOK), BF16), pltpu.VMEM((CHUNKS, DEVS, 2, CC, TOK), BF16),
            pltpu.VMEM((DEVS * 2 * CC, TOK), F32), pltpu.VMEM((DEVS * CC, TOK), F32),
            pltpu.VMEM((CHUNKS, DEVS, CC, TOK), BF16), pltpu.VMEM((CHUNKS, DEVS, CC, TOK), BF16),
            pltpu.SemaphoreType.DMA((10,)), pltpu.SemaphoreType.DMA((CHUNKS,)),
            pltpu.SemaphoreType.DMA((CHUNKS,)), pltpu.SemaphoreType.DMA((CHUNKS,)), pltpu.SemaphoreType.DMA((CHUNKS,)),
            pltpu.SemaphoreType.DMA((CHUNKS,)), pltpu.SemaphoreType.DMA((CHUNKS,)), pltpu.SemaphoreType.DMA((CHUNKS,)),
        ],
        compiler_params=pltpu.CompilerParams(
            collective_id=0, has_side_effects=True, vmem_limit_bytes=60 << 20
        ),
        cost_estimate=pl.CostEstimate(flops=3 << 30, bytes_accessed=6 << 20, transcendentals=0),
        name="long_conv",
    )(query_proj, key_proj, value_proj, filter_taps, skip_gain.reshape(1, 4096), *(jnp.asarray(t) for t in tables()))


def solution(mesh):
    split = P(("seq", "chan"), None)
    return jax.shard_map(
        shards, mesh=mesh, in_specs=(split, split, split, split, P()), out_specs=split, check_vma=False
    )
```

```python
import functools
import math

import jax
import jax.numpy as jnp
import numpy as np
from jax import lax
from jax.experimental import pallas as pl
from jax.experimental.pallas import tpu as pltpu
from jax.sharding import PartitionSpec as P

MESH = pl.DeviceIdType.MESH
DEVS = 128
TOK = 128
CHUNKS = 2
CC = 16
BATCH = 16
UNROLL = 4
BLOCKS = 16
F32 = jnp.float32
BF16 = jnp.bfloat16


def tables():
    idx = np.arange(128)
    coarse = 2.0 * math.pi * np.outer(idx + 0.5, idx) / 256.0
    twist = 2.0 * math.pi * np.outer(idx + 0.5, idx) / 32768.0
    inner = 2.0 * math.pi * (np.outer(idx, idx) % 128) / 128.0
    fwd_outer = np.concatenate([np.cos(coarse), -np.sin(coarse)], axis=0)
    cos_in, sin_in = np.cos(inner), np.sin(inner)
    fwd_inner = np.block([[cos_in, -sin_in], [sin_in, cos_in]])
    inv_inner = np.block([[cos_in, sin_in], [-sin_in, cos_in]])
    inv_outer = np.concatenate([np.cos(coarse.T), -np.sin(coarse.T)], axis=1) * (2.0 / 32768.0)
    twists = np.stack([np.cos(twist), -np.sin(twist)])
    return (
        fwd_outer.astype(jnp.bfloat16),
        fwd_inner.astype(jnp.bfloat16),
        inv_inner.astype(jnp.bfloat16),
        inv_outer.astype(jnp.bfloat16),
        twists.astype(np.float32),
    )


def sweep(visit):
    seq, chan = lax.axis_index("seq"), lax.axis_index("chan")
    here = (chan // 4, seq // 2, chan % 4)
    cores = (seq % 2, 1 - seq % 2)
    fixed = [[lax.rem(at + far, 4) for far in range(4)] for at in here]

    def go(place, core):
        seq_to, chan_to = place[1] * 2 + cores[core], place[0] * 4 + place[2]
        visit(seq_to * 16 + chan_to, (seq_to, chan_to))

    def moving(turn):
        fars = (turn + 1, lax.rem(turn + 1, 3) + 1, lax.rem(turn + 2, 3) + 1)
        return [[lax.rem(at + far, 4) for far in fars] for at in here]

    def three_axes(turn, carry):
        moved = moving(turn)
        for a in range(3):
            for b in range(3):
                for core in range(2):
                    go((moved[0][(a + b) % 3], fixed[1][(2, 1, 3)[a]], fixed[2][(2, 1, 3)[b]]), core)
        return carry

    def two_axes(turn, carry):
        moved = moving(turn)
        for a in range(3):
            for still in range(3):
                place = [at for at in here]
                place[(still + 1) % 3] = fixed[(still + 1) % 3][(2, 1, 3)[a]]
                place[(still + 2) % 3] = moved[(still + 2) % 3][(a + still) % 3]
                for core in range(2):
                    go(place, core)
        return carry

    def one_axis(turn, carry):
        moved = moving(turn)
        for axis in range(3):
            place = [at for at in here]
            place[axis] = moved[axis][axis]
            for core in range(2):
                go(place, core)
        return carry

    for walk in (three_axes, two_axes, one_axis):
        lax.fori_loop(0, 3, walk, 0)
    go(here, 1)


def kernel(
    q_hbm, k_hbm, v_hbm, h_hbm, gain_hbm, fo_hbm, fi_hbm, ii_hbm, io_hbm, tw_hbm, out_hbm,
    q_buf, k_buf, v_buf, h_buf, gain_buf, fo_buf, fi_buf, ii_buf, io_buf, tw_buf, out_buf,
    send, recv, wide, tap_spec, ywide, ysend, yrecv,
    in_sem, out_sem, send_sem, recv_sem, ysend_sem, yrecv_sem,
):
    seq, chan = lax.axis_index("seq"), lax.axis_index("chan")
    me = seq * 16 + chan

    pairs = (
        (h_hbm, h_buf), (k_hbm, k_buf), (v_hbm, v_buf), (fo_hbm, fo_buf), (fi_hbm, fi_buf), (ii_hbm, ii_buf),
        (io_hbm, io_buf), (tw_hbm, tw_buf), (q_hbm, q_buf), (gain_hbm, gain_buf),
    )
    loads = [pltpu.make_async_copy(src, dst, in_sem.at[i]) for i, (src, dst) in enumerate(pairs)]
    for load in loads:
        load.start()

    barrier = pltpu.get_barrier_semaphore()
    sweep(lambda peer, place: pl.semaphore_signal(barrier, inc=1, device_id=place, device_id_type=MESH))

    def lanes_of(chunk, block):
        return pl.ds(pl.multiple_of(chunk * (BLOCKS * 128) + block * 128, 128), 128)

    def pack_taps(chunk, block, carry):
        send[chunk, pl.ds(block * 8, 8)] = h_buf[:, lanes_of(chunk, block)].T.reshape(8, CC, TOK)
        return carry

    def pack_product(chunk, block, carry):
        lanes = lanes_of(chunk, block)
        product = (k_buf[:, lanes].astype(F32) * v_buf[:, lanes].astype(F32)).astype(BF16)
        send[CHUNKS + chunk, pl.ds(block * 8, 8)] = product.T.reshape(8, CC, TOK)
        return carry

    def give(piece):
        def visit(peer, place):
            pltpu.make_async_remote_copy(
                src_ref=send.at[piece, peer], dst_ref=recv.at[piece, me],
                send_sem=send_sem.at[piece], recv_sem=recv_sem.at[piece],
                device_id=place, device_id_type=MESH,
            ).start()

        sweep(visit)
        recv[piece, me] = send[piece, me]

    loads[0].wait()
    for chunk in range(CHUNKS):
        lax.fori_loop(0, BLOCKS, functools.partial(pack_taps, chunk), 0, unroll=UNROLL)
    loads[1].wait()
    loads[2].wait()
    lax.fori_loop(0, BLOCKS, functools.partial(pack_product, 0), 0, unroll=UNROLL)
    pl.semaphore_wait(barrier, DEVS - 1)
    for piece in range(CHUNKS + 1):
        give(piece)
    lax.fori_loop(0, BLOCKS, functools.partial(pack_product, 1), 0, unroll=UNROLL)
    give(CHUNKS + 1)
    for load in loads[3:]:
        load.wait()

    others = pl.ds(0, DEVS - 1)

    def widen(piece, step, carry):
        rows = pl.ds(pl.multiple_of(step * (16 * CC), 16 * CC), 16 * CC)
        wide[rows, :] = recv[piece, pl.ds(step * 16, 16)].reshape(16 * CC, TOK).astype(F32)
        return carry

    def spectra(first):
        twist_re, twist_im = tw_buf[0], tw_buf[1]
        rows = []
        for c in range(0, BATCH, 2):
            both = jnp.concatenate(
                [wide[pl.ds(first + c + odd, DEVS, CC), :].astype(BF16) for odd in range(2)], axis=1)
            both = jnp.dot(fo_buf[...], both, preferred_element_type=F32)
            for lane in (0, 128):
                re, im = both[:128, lane:lane + 128], both[128:, lane:lane + 128]
                rows.append(jnp.concatenate(
                    [(re * twist_re - im * twist_im).astype(BF16), (re * twist_im + im * twist_re).astype(BF16)], axis=1))
        return jnp.dot(jnp.concatenate(rows, axis=0), fi_buf[...], preferred_element_type=F32)

    def transform_taps(chunk, at, carry):
        rows = pl.ds(pl.multiple_of((chunk * CC + at * BATCH) * 128, 128), BATCH * 128)
        tap_spec[rows, :] = spectra(at * BATCH)
        return carry

    def convolve(chunk, at, carry):
        twist_re, twist_im = tw_buf[0], tw_buf[1]
        x_all = spectra(at * BATCH)
        products = []
        for c in range(BATCH):
            taps = tap_spec[pl.ds(pl.multiple_of((chunk * CC + at * BATCH + c) * 128, 128), 128), :]
            x_re, x_im = x_all[c * 128:c * 128 + 128, :128], x_all[c * 128:c * 128 + 128, 128:]
            h_re, h_im = taps[:, :128], taps[:, 128:]
            products.append(jnp.concatenate(
                [(x_re * h_re - x_im * h_im).astype(BF16), (x_re * h_im + x_im * h_re).astype(BF16)], axis=1))
        back = jnp.dot(jnp.concatenate(products, axis=0), ii_buf[...], preferred_element_type=F32)
        turned = []
        for c in range(BATCH):
            re, im = back[c * 128:c * 128 + 128, :128], back[c * 128:c * 128 + 128, 128:]
            turned.append(jnp.concatenate(
                [(re * twist_re + im * twist_im).astype(BF16), (im * twist_re - re * twist_im).astype(BF16)], axis=0))
        for c in range(0, BATCH, 2):
            y = jnp.dot(io_buf[...], jnp.concatenate(turned[c:c + 2], axis=1), preferred_element_type=F32)
            ywide[pl.ds(BATCH * at + c, DEVS, CC), :] = y[:, :128]
            ywide[pl.ds(BATCH * at + c + 1, DEVS, CC), :] = y[:, 128:]
        return carry

    def narrow(chunk, step, carry):
        rows = pl.ds(pl.multiple_of(step * (16 * CC), 16 * CC), 16 * CC)
        ysend[chunk, pl.ds(step * 16, 16)] = ywide[rows, :].astype(BF16).reshape(16, CC, TOK)
        return carry

    def give_back(chunk):
        def visit(peer, place):
            pltpu.make_async_remote_copy(
                src_ref=ysend.at[chunk, peer], dst_ref=yrecv.at[chunk, me],
                send_sem=ysend_sem.at[chunk], recv_sem=yrecv_sem.at[chunk],
                device_id=place, device_id_type=MESH,
            ).start()

        sweep(visit)
        yrecv[chunk, me] = ysend[chunk, me]

    for piece in range(2 * CHUNKS):
        chunk = piece % CHUNKS
        arrived = recv.at[piece, others]
        pltpu.make_async_copy(arrived, arrived, recv_sem.at[piece]).wait()
        lax.fori_loop(0, 8, functools.partial(widen, piece), 0)
        if piece < CHUNKS:
            lax.fori_loop(0, CC // BATCH, functools.partial(transform_taps, chunk), 0)
        else:
            lax.fori_loop(0, CC // BATCH, functools.partial(convolve, chunk), 0)
            lax.fori_loop(0, 8, functools.partial(narrow, chunk), 0)
            give_back(chunk)

    def gate(chunk, block, carry):
        lanes = lanes_of(chunk, block)
        convolved = yrecv[chunk, pl.ds(block * 8, 8)].reshape(128, TOK).T.astype(F32)
        product = (k_buf[:, lanes].astype(F32) * v_buf[:, lanes].astype(F32)).astype(BF16).astype(F32)
        out_buf[:, lanes] = (q_buf[:, lanes].astype(F32) * (convolved + gain_buf[:, lanes] * product)).astype(BF16)
        return carry

    stores = []
    for chunk in range(CHUNKS):
        arrived = yrecv.at[chunk, others]
        pltpu.make_async_copy(arrived, arrived, yrecv_sem.at[chunk]).wait()
        lax.fori_loop(0, BLOCKS, functools.partial(gate, chunk), 0, unroll=UNROLL)
        half = pl.ds(chunk * BLOCKS * 128, BLOCKS * 128)
        stores.append(pltpu.make_async_copy(out_buf.at[:, half], out_hbm.at[:, half], out_sem.at[chunk]))
        stores[-1].start()
    for store in stores:
        store.wait()
    for piece in range(2 * CHUNKS):
        left = send.at[piece, others]
        pltpu.make_async_copy(left, left, send_sem.at[piece]).wait()
    for chunk in range(CHUNKS):
        left = ysend.at[chunk, others]
        pltpu.make_async_copy(left, left, ysend_sem.at[chunk]).wait()


def shards(query_proj, key_proj, value_proj, filter_taps, skip_gain):
    whole = (TOK, 4096)
    any_spec = pl.BlockSpec(memory_space=pltpu.HBM)
    return pl.pallas_call(
        kernel,
        out_shape=jax.ShapeDtypeStruct(whole, BF16),
        in_specs=[any_spec] * 10,
        out_specs=pl.BlockSpec(memory_space=pl.ANY),
        scratch_shapes=[
            pltpu.VMEM(whole, BF16), pltpu.VMEM(whole, BF16), pltpu.VMEM(whole, BF16), pltpu.VMEM(whole, BF16),
            pltpu.VMEM((1, 4096), F32),
            pltpu.VMEM((256, 128), BF16), pltpu.VMEM((256, 256), BF16), pltpu.VMEM((256, 256), BF16),
            pltpu.VMEM((128, 256), BF16), pltpu.VMEM((2, 128, 128), F32),
            pltpu.VMEM(whole, BF16),
            pltpu.VMEM((2 * CHUNKS, DEVS, CC, TOK), BF16), pltpu.VMEM((2 * CHUNKS, DEVS, CC, TOK), BF16),
            pltpu.VMEM((DEVS * CC, TOK), F32), pltpu.VMEM((CHUNKS * CC * 128, 256), F32), pltpu.VMEM((DEVS * CC, TOK), F32),
            pltpu.VMEM((CHUNKS, DEVS, CC, TOK), BF16), pltpu.VMEM((CHUNKS, DEVS, CC, TOK), BF16),
            pltpu.SemaphoreType.DMA((10,)), pltpu.SemaphoreType.DMA((CHUNKS,)),
            pltpu.SemaphoreType.DMA((2 * CHUNKS,)), pltpu.SemaphoreType.DMA((2 * CHUNKS,)),
            pltpu.SemaphoreType.DMA((CHUNKS,)), pltpu.SemaphoreType.DMA((CHUNKS,)),
        ],
        compiler_params=pltpu.CompilerParams(
            collective_id=0, has_side_effects=True, vmem_limit_bytes=60 << 20
        ),
        cost_estimate=pl.CostEstimate(flops=3 << 30, bytes_accessed=6 << 20, transcendentals=0),
        name="long_conv",
    )(query_proj, key_proj, value_proj, filter_taps, skip_gain.reshape(1, 4096), *(jnp.asarray(t) for t in tables()))


def solution(mesh):
    split = P(("seq", "chan"), None)
    return jax.shard_map(
        shards, mesh=mesh, in_specs=(split, split, split, split, P()), out_specs=split, check_vma=False
    )
```

```python
import functools
import math

import jax
import jax.numpy as jnp
import numpy as np
from jax import lax
from jax.experimental import pallas as pl
from jax.experimental.pallas import tpu as pltpu
from jax.sharding import PartitionSpec as P

MESH = pl.DeviceIdType.MESH
DEVS = 128
TOK = 128
CHUNKS = 2
CC = 16
BATCH = 16
UNROLL = 4
BLOCKS = 16
F32 = jnp.float32
BF16 = jnp.bfloat16


def tables():
    idx = np.arange(128)
    coarse = 2.0 * math.pi * np.outer(idx + 0.5, idx) / 256.0
    twist = 2.0 * math.pi * np.outer(idx + 0.5, idx) / 32768.0
    inner = 2.0 * math.pi * (np.outer(idx, idx) % 128) / 128.0
    fwd_outer = np.concatenate([np.cos(coarse), -np.sin(coarse)], axis=0)
    cos_in, sin_in = np.cos(inner), np.sin(inner)
    fwd_inner = np.block([[cos_in, -sin_in], [sin_in, cos_in]])
    inv_inner = np.block([[cos_in, sin_in], [-sin_in, cos_in]])
    inv_outer = np.concatenate([np.cos(coarse.T), -np.sin(coarse.T)], axis=1) * (2.0 / 32768.0)
    twists = np.stack([np.cos(twist), -np.sin(twist)])
    return (
        fwd_outer.astype(jnp.bfloat16),
        fwd_inner.astype(jnp.bfloat16),
        inv_inner.astype(jnp.bfloat16),
        inv_outer.astype(jnp.bfloat16),
        twists.astype(np.float32),
    )


STEPS = (
    84, 85, 86, 116, 77, 52, 87, 76, 93, 117, 83, 53, 92, 82, 45, 54,
    74, 91, 20, 95, 60, 75, 55, 109, 119, 79, 61, 115, 90, 124, 80, 125,
    118, 94, 44, 78, 21, 81, 108, 69, 114, 50, 68, 51, 42, 122, 43, 111,
    123, 63, 106, 62, 59, 46, 107, 126, 58, 47, 127, 110, 12, 72, 22, 70,
    13, 73, 101, 112, 19, 67, 18, 71, 29, 88, 49, 36, 28, 89, 66, 23,
    48, 100, 113, 37, 15, 102, 121, 98, 27, 120, 30, 40, 39, 99, 104, 31,
    38, 105, 14, 103, 11, 41, 34, 17, 35, 56, 10, 5, 64, 57, 26, 16,
    4, 65, 97, 9, 7, 8, 96, 3, 6, 25, 32, 2, 24, 33, 1,
)


def sweep(visit):
    seq, chan = lax.axis_index("seq"), lax.axis_index("chan")
    sense = 1 + 2 * (seq % 2)
    x, y, z = ([lax.rem(at + far * sense, 4) for far in range(4)] for at in (chan // 4, seq // 2, chan % 4))
    cores = (seq % 2, 1 - seq % 2)
    for code in STEPS:
        seq_to = y[code // 8 % 4] * 2 + cores[code % 2]
        chan_to = x[code // 32] * 4 + z[code // 2 % 4]
        visit(seq_to * 16 + chan_to, (seq_to, chan_to))


def kernel(
    q_hbm, k_hbm, v_hbm, h_hbm, gain_hbm, fo_hbm, fi_hbm, ii_hbm, io_hbm, tw_hbm, out_buf,
    q_buf, k_buf, v_buf, h_buf, gain_buf, fo_buf, fi_buf, ii_buf, io_buf, tw_buf,
    send, recv, wide, tap_spec, ywide, ysend, yrecv,
    in_sem, send_sem, recv_sem, ysend_sem, yrecv_sem,
):
    seq, chan = lax.axis_index("seq"), lax.axis_index("chan")
    me = seq * 16 + chan

    pairs = (
        (h_hbm, h_buf), (k_hbm, k_buf), (v_hbm, v_buf), (fo_hbm, fo_buf), (fi_hbm, fi_buf), (ii_hbm, ii_buf),
        (io_hbm, io_buf), (tw_hbm, tw_buf), (q_hbm, q_buf), (gain_hbm, gain_buf),
    )
    loads = [pltpu.make_async_copy(src, dst, in_sem.at[i]) for i, (src, dst) in enumerate(pairs)]
    for load in loads:
        load.start()

    barrier = pltpu.get_barrier_semaphore()
    sweep(lambda peer, place: pl.semaphore_signal(barrier, inc=1, device_id=place, device_id_type=MESH))

    def lanes_of(chunk, block):
        return pl.ds(pl.multiple_of(chunk * (BLOCKS * 128) + block * 128, 128), 128)

    def pack_taps(chunk, block, carry):
        send[chunk, pl.ds(block * 8, 8)] = h_buf[:, lanes_of(chunk, block)].T.reshape(8, CC, TOK)
        return carry

    def pack_product(chunk, block, carry):
        lanes = lanes_of(chunk, block)
        product = (k_buf[:, lanes].astype(F32) * v_buf[:, lanes].astype(F32)).astype(BF16)
        send[CHUNKS + chunk, pl.ds(block * 8, 8)] = product.T.reshape(8, CC, TOK)
        return carry

    def give(piece):
        def visit(peer, place):
            pltpu.make_async_remote_copy(
                src_ref=send.at[piece, peer], dst_ref=recv.at[piece, me],
                send_sem=send_sem.at[piece], recv_sem=recv_sem.at[piece],
                device_id=place, device_id_type=MESH,
            ).start()

        sweep(visit)

    loads[0].wait()
    for chunk in range(CHUNKS):
        lax.fori_loop(0, BLOCKS, functools.partial(pack_taps, chunk), 0, unroll=UNROLL)
    pl.semaphore_wait(barrier, DEVS - 1)
    loads[1].wait()
    loads[2].wait()
    lax.fori_loop(0, BLOCKS, functools.partial(pack_product, 0), 0, unroll=UNROLL)

    @pl.loop(0, CHUNKS + 1)
    def _(piece):
        give(piece)

    lax.fori_loop(0, BLOCKS, functools.partial(pack_product, 1), 0, unroll=UNROLL)
    give(CHUNKS + 1)
    for piece in range(2 * CHUNKS):
        recv[piece, me] = send[piece, me]
    for load in loads[3:]:
        load.wait()

    others = pl.ds(0, DEVS - 1)

    def widen(piece, step, carry):
        rows = pl.ds(pl.multiple_of(step * (16 * CC), 16 * CC), 16 * CC)
        wide[rows, :] = recv[piece, pl.ds(step * 16, 16)].reshape(16 * CC, TOK).astype(F32)
        return carry

    def spectra(first):
        twist_re, twist_im = tw_buf[0], tw_buf[1]
        rows = []
        for c in range(0, BATCH, 2):
            both = jnp.concatenate(
                [wide[pl.ds(first + c + odd, DEVS, CC), :].astype(BF16) for odd in range(2)], axis=1)
            both = jnp.dot(fo_buf[...], both, preferred_element_type=F32)
            for lane in (0, 128):
                re, im = both[:128, lane:lane + 128], both[128:, lane:lane + 128]
                rows.append(jnp.concatenate(
                    [(re * twist_re - im * twist_im).astype(BF16), (re * twist_im + im * twist_re).astype(BF16)], axis=1))
        return jnp.dot(jnp.concatenate(rows, axis=0), fi_buf[...], preferred_element_type=F32)

    def transform_taps(chunk, at, carry):
        rows = pl.ds(pl.multiple_of((chunk * CC + at * BATCH) * 128, 128), BATCH * 128)
        tap_spec[rows, :] = spectra(at * BATCH)
        return carry

    def convolve(chunk, at, carry):
        twist_re, twist_im = tw_buf[0], tw_buf[1]
        x_all = spectra(at * BATCH)
        products = []
        for c in range(BATCH):
            taps = tap_spec[pl.ds(pl.multiple_of((chunk * CC + at * BATCH + c) * 128, 128), 128), :]
            x_re, x_im = x_all[c * 128:c * 128 + 128, :128], x_all[c * 128:c * 128 + 128, 128:]
            h_re, h_im = taps[:, :128], taps[:, 128:]
            products.append(jnp.concatenate(
                [(x_re * h_re - x_im * h_im).astype(BF16), (x_re * h_im + x_im * h_re).astype(BF16)], axis=1))
        back = jnp.dot(jnp.concatenate(products, axis=0), ii_buf[...], preferred_element_type=F32)
        turned = []
        for c in range(BATCH):
            re, im = back[c * 128:c * 128 + 128, :128], back[c * 128:c * 128 + 128, 128:]
            turned.append(jnp.concatenate(
                [(re * twist_re + im * twist_im).astype(BF16), (im * twist_re - re * twist_im).astype(BF16)], axis=0))
        for c in range(0, BATCH, 2):
            y = jnp.dot(io_buf[...], jnp.concatenate(turned[c:c + 2], axis=1), preferred_element_type=F32)
            ywide[pl.ds(BATCH * at + c, DEVS, CC), :] = y[:, :128]
            ywide[pl.ds(BATCH * at + c + 1, DEVS, CC), :] = y[:, 128:]
        return carry

    def narrow(chunk, step, carry):
        rows = pl.ds(pl.multiple_of(step * (16 * CC), 16 * CC), 16 * CC)
        ysend[chunk, pl.ds(step * 16, 16)] = ywide[rows, :].astype(BF16).reshape(16, CC, TOK)
        return carry

    def give_back(chunk):
        def visit(peer, place):
            pltpu.make_async_remote_copy(
                src_ref=ysend.at[chunk, peer], dst_ref=yrecv.at[chunk, me],
                send_sem=ysend_sem.at[chunk], recv_sem=yrecv_sem.at[chunk],
                device_id=place, device_id_type=MESH,
            ).start()

        sweep(visit)
        yrecv[chunk, me] = ysend[chunk, me]

    def take(piece):
        arrived = recv.at[piece, others]
        pltpu.make_async_copy(arrived, arrived, recv_sem.at[piece]).wait()
        lax.fori_loop(0, 8, functools.partial(widen, piece), 0)

    @pl.loop(0, CHUNKS)
    def _(chunk):
        take(chunk)
        lax.fori_loop(0, CC // BATCH, functools.partial(transform_taps, chunk), 0)

    @pl.loop(0, CHUNKS)
    def _(chunk):
        take(CHUNKS + chunk)
        lax.fori_loop(0, CC // BATCH, functools.partial(convolve, chunk), 0)
        lax.fori_loop(0, 8, functools.partial(narrow, chunk), 0)
        give_back(chunk)

    def gate(chunk, block, carry):
        lanes = lanes_of(chunk, block)
        convolved = yrecv[chunk, pl.ds(block * 8, 8)].reshape(128, TOK).T.astype(F32)
        product = (k_buf[:, lanes].astype(F32) * v_buf[:, lanes].astype(F32)).astype(BF16).astype(F32)
        out_buf[:, lanes] = (q_buf[:, lanes].astype(F32) * (convolved + gain_buf[:, lanes] * product)).astype(BF16)
        return carry

    for chunk in range(CHUNKS):
        arrived = yrecv.at[chunk, others]
        pltpu.make_async_copy(arrived, arrived, yrecv_sem.at[chunk]).wait()
        lax.fori_loop(0, BLOCKS, functools.partial(gate, chunk), 0, unroll=UNROLL)
    for piece in range(2 * CHUNKS):
        left = send.at[piece, others]
        pltpu.make_async_copy(left, left, send_sem.at[piece]).wait()
    for chunk in range(CHUNKS):
        left = ysend.at[chunk, others]
        pltpu.make_async_copy(left, left, ysend_sem.at[chunk]).wait()


def shards(query_proj, key_proj, value_proj, filter_taps, skip_gain):
    whole = (TOK, 4096)
    held = [
        pltpu.with_memory_space_constraint(a, pltpu.HBM)
        for a in (query_proj, key_proj, value_proj, filter_taps, skip_gain.reshape(1, 4096), *map(jnp.asarray, tables()))
    ]
    return pl.pallas_call(
        kernel,
        out_shape=pltpu.VMEM(whole, BF16),
        in_specs=[pl.BlockSpec(memory_space=pltpu.HBM)] * len(held),
        out_specs=pl.BlockSpec(memory_space=pltpu.VMEM),
        scratch_shapes=[
            pltpu.VMEM(whole, BF16), pltpu.VMEM(whole, BF16), pltpu.VMEM(whole, BF16), pltpu.VMEM(whole, BF16),
            pltpu.VMEM((1, 4096), F32),
            pltpu.VMEM((256, 128), BF16), pltpu.VMEM((256, 256), BF16), pltpu.VMEM((256, 256), BF16),
            pltpu.VMEM((128, 256), BF16), pltpu.VMEM((2, 128, 128), F32),
            pltpu.VMEM((2 * CHUNKS, DEVS, CC, TOK), BF16), pltpu.VMEM((2 * CHUNKS, DEVS, CC, TOK), BF16),
            pltpu.VMEM((DEVS * CC, TOK), F32), pltpu.VMEM((CHUNKS * CC * 128, 256), F32), pltpu.VMEM((DEVS * CC, TOK), F32),
            pltpu.VMEM((CHUNKS, DEVS, CC, TOK), BF16), pltpu.VMEM((CHUNKS, DEVS, CC, TOK), BF16),
            pltpu.SemaphoreType.DMA((10,)),
            pltpu.SemaphoreType.DMA((2 * CHUNKS,)), pltpu.SemaphoreType.DMA((2 * CHUNKS,)),
            pltpu.SemaphoreType.DMA((CHUNKS,)), pltpu.SemaphoreType.DMA((CHUNKS,)),
        ],
        compiler_params=pltpu.CompilerParams(
            collective_id=0, has_side_effects=True, vmem_limit_bytes=48 << 20
        ),
        cost_estimate=pl.CostEstimate(flops=3 << 30, bytes_accessed=6 << 20, transcendentals=0),
        name="long_conv",
    )(*held)


def solution(mesh):
    split = P(("seq", "chan"), None)
    return jax.shard_map(
        shards, mesh=mesh, in_specs=(split, split, split, split, P()), out_specs=split, check_vma=False
    )
```

```python
import functools
import math

import jax
import jax.numpy as jnp
import numpy as np
from jax import lax
from jax.experimental import pallas as pl
from jax.experimental.pallas import tpu as pltpu
from jax.sharding import PartitionSpec as P

MESH = pl.DeviceIdType.MESH
DEVS = 128
TOK = 128
CHUNKS = 2
CC = 16
BATCH = 16
UNROLL = 4
BLOCKS = 16
F32 = jnp.float32
BF16 = jnp.bfloat16


def tables():
    idx = np.arange(128)
    coarse = 2.0 * math.pi * np.outer(idx + 0.5, idx) / 256.0
    twist = 2.0 * math.pi * np.outer(idx + 0.5, idx) / 32768.0
    inner = 2.0 * math.pi * (np.outer(idx, idx) % 128) / 128.0
    fwd_outer = np.concatenate([np.cos(coarse), -np.sin(coarse)], axis=0)
    cos_in, sin_in = np.cos(inner), np.sin(inner)
    fwd_inner = np.block([[cos_in, -sin_in], [sin_in, cos_in]])
    inv_inner = np.block([[cos_in, sin_in], [-sin_in, cos_in]])
    inv_outer = np.concatenate([np.cos(coarse.T), -np.sin(coarse.T)], axis=1) * (2.0 / 32768.0)
    twists = np.stack([np.cos(twist), -np.sin(twist)])
    return (
        fwd_outer.astype(jnp.bfloat16),
        fwd_inner.astype(jnp.bfloat16),
        inv_inner.astype(jnp.bfloat16),
        inv_outer.astype(jnp.bfloat16),
        twists.astype(np.float32),
    )


STEPS = (
    84, 85, 86, 116, 77, 52, 87, 76, 93, 117, 83, 53, 92, 82, 45, 54,
    74, 91, 20, 95, 60, 75, 55, 109, 119, 79, 61, 115, 90, 124, 80, 125,
    118, 94, 44, 78, 21, 81, 108, 69, 114, 50, 68, 51, 42, 122, 43, 111,
    123, 63, 106, 62, 59, 46, 107, 126, 58, 47, 127, 110, 12, 72, 22, 70,
    13, 73, 101, 112, 19, 67, 18, 71, 29, 88, 49, 36, 28, 89, 66, 23,
    48, 100, 113, 37, 15, 102, 121, 98, 27, 120, 30, 40, 39, 99, 104, 31,
    38, 105, 14, 103, 11, 41, 34, 17, 35, 56, 10, 5, 64, 57, 26, 16,
    4, 65, 97, 9, 7, 8, 96, 3, 6, 25, 32, 2, 24, 33, 1,
)


def sweep(visit):
    seq, chan = lax.axis_index("seq"), lax.axis_index("chan")
    sense = 1 + 2 * (seq % 2)
    x, y, z = ([lax.rem(at + far * sense, 4) for far in range(4)] for at in (chan // 4, seq // 2, chan % 4))
    cores = (seq % 2, 1 - seq % 2)
    for code in STEPS:
        seq_to = y[code // 8 % 4] * 2 + cores[code % 2]
        chan_to = x[code // 32] * 4 + z[code // 2 % 4]
        visit(seq_to * 16 + chan_to, (seq_to, chan_to))


def kernel(
    q_hbm, k_hbm, v_hbm, h_hbm, gain_hbm, fo_hbm, fi_hbm, ii_hbm, io_hbm, tw_hbm, out_buf,
    q_buf, k_buf, v_buf, h_buf, gain_buf, fo_buf, fi_buf, ii_buf, io_buf, tw_buf,
    send, recv, wide, tap_spec, ywide, ysend, yrecv,
    in_sem, send_sem, recv_sem, ysend_sem, yrecv_sem,
):
    seq, chan = lax.axis_index("seq"), lax.axis_index("chan")
    me = seq * 16 + chan

    pairs = (
        (h_hbm, h_buf), (k_hbm, k_buf), (v_hbm, v_buf), (fo_hbm, fo_buf), (fi_hbm, fi_buf), (ii_hbm, ii_buf),
        (io_hbm, io_buf), (tw_hbm, tw_buf), (q_hbm, q_buf), (gain_hbm, gain_buf),
    )
    loads = [pltpu.make_async_copy(src, dst, in_sem.at[i]) for i, (src, dst) in enumerate(pairs)]
    for i, load in enumerate(loads):
        if i < 3:
            for part in range(4):
                rows = pl.ds(part * (TOK // 4), TOK // 4)
                pltpu.make_async_copy(pairs[i][0].at[rows], pairs[i][1].at[rows], in_sem.at[i]).start()
        else:
            load.start()

    barrier = pltpu.get_barrier_semaphore()
    sweep(lambda peer, place: pl.semaphore_signal(barrier, inc=1, device_id=place, device_id_type=MESH))

    def lanes_of(chunk, block):
        return pl.ds(pl.multiple_of(chunk * (BLOCKS * 128) + block * 128, 128), 128)

    def pack_taps(chunk, block, carry):
        send[chunk, pl.ds(block * 8, 8)] = h_buf[:, lanes_of(chunk, block)].T.reshape(8, CC, TOK)
        return carry

    def pack_product(chunk, block, carry):
        lanes = lanes_of(chunk, block)
        product = (k_buf[:, lanes].astype(F32) * v_buf[:, lanes].astype(F32)).astype(BF16)
        send[CHUNKS + chunk, pl.ds(block * 8, 8)] = product.T.reshape(8, CC, TOK)
        return carry

    def give(piece):
        def visit(peer, place):
            pltpu.make_async_remote_copy(
                src_ref=send.at[piece, peer], dst_ref=recv.at[piece, me],
                send_sem=send_sem.at[piece], recv_sem=recv_sem.at[piece],
                device_id=place, device_id_type=MESH,
            ).start()

        sweep(visit)

    def pack(body):
        lax.fori_loop(0, BLOCKS, body, 0, unroll=UNROLL)

    loads[0].wait()
    pack(functools.partial(pack_taps, 0))
    pl.semaphore_wait(barrier, DEVS - 1)

    @pl.loop(0, 2 * CHUNKS)
    def _(piece):
        @pl.when(piece == 1)
        def _():
            pack(functools.partial(pack_taps, 1))

        @pl.when(piece == CHUNKS)
        def _():
            loads[1].wait()
            loads[2].wait()

        @pl.when(piece >= CHUNKS)
        def _():
            pack(functools.partial(pack_product, piece - CHUNKS))

        give(piece)

    for piece in range(2 * CHUNKS):
        recv[piece, me] = send[piece, me]
    for load in loads[3:]:
        load.wait()

    others = pl.ds(0, DEVS - 1)

    def widen(piece, step, carry):
        rows = pl.ds(pl.multiple_of(step * (16 * CC), 16 * CC), 16 * CC)
        wide[rows, :] = recv[piece, pl.ds(step * 16, 16)].reshape(16 * CC, TOK).astype(F32)
        return carry

    def spectra(first):
        twist_re, twist_im = tw_buf[0], tw_buf[1]
        rows = []
        for c in range(0, BATCH, 2):
            both = jnp.concatenate(
                [wide[pl.ds(first + c + odd, DEVS, CC), :].astype(BF16) for odd in range(2)], axis=1)
            both = jnp.dot(fo_buf[...], both, preferred_element_type=F32)
            for lane in (0, 128):
                re, im = both[:128, lane:lane + 128], both[128:, lane:lane + 128]
                rows.append(jnp.concatenate(
                    [(re * twist_re - im * twist_im).astype(BF16), (re * twist_im + im * twist_re).astype(BF16)], axis=1))
        return jnp.dot(jnp.concatenate(rows, axis=0), fi_buf[...], preferred_element_type=F32)

    def transform_taps(chunk, at, carry):
        rows = pl.ds(pl.multiple_of((chunk * CC + at * BATCH) * 128, 128), BATCH * 128)
        tap_spec[rows, :] = spectra(at * BATCH)
        return carry

    def convolve(chunk, at, carry):
        twist_re, twist_im = tw_buf[0], tw_buf[1]
        x_all = spectra(at * BATCH)
        products = []
        for c in range(BATCH):
            taps = tap_spec[pl.ds(pl.multiple_of((chunk * CC + at * BATCH + c) * 128, 128), 128), :]
            x_re, x_im = x_all[c * 128:c * 128 + 128, :128], x_all[c * 128:c * 128 + 128, 128:]
            h_re, h_im = taps[:, :128], taps[:, 128:]
            products.append(jnp.concatenate(
                [(x_re * h_re - x_im * h_im).astype(BF16), (x_re * h_im + x_im * h_re).astype(BF16)], axis=1))
        back = jnp.dot(jnp.concatenate(products, axis=0), ii_buf[...], preferred_element_type=F32)
        turned = []
        for c in range(BATCH):
            re, im = back[c * 128:c * 128 + 128, :128], back[c * 128:c * 128 + 128, 128:]
            turned.append(jnp.concatenate(
                [(re * twist_re + im * twist_im).astype(BF16), (im * twist_re - re * twist_im).astype(BF16)], axis=0))
        for c in range(0, BATCH, 2):
            y = jnp.dot(io_buf[...], jnp.concatenate(turned[c:c + 2], axis=1), preferred_element_type=F32)
            ywide[pl.ds(BATCH * at + c, DEVS, CC), :] = y[:, :128]
            ywide[pl.ds(BATCH * at + c + 1, DEVS, CC), :] = y[:, 128:]
        return carry

    def narrow(chunk, step, carry):
        rows = pl.ds(pl.multiple_of(step * (16 * CC), 16 * CC), 16 * CC)
        ysend[chunk, pl.ds(step * 16, 16)] = ywide[rows, :].astype(BF16).reshape(16, CC, TOK)
        return carry

    def give_back(chunk):
        def visit(peer, place):
            pltpu.make_async_remote_copy(
                src_ref=ysend.at[chunk, peer], dst_ref=yrecv.at[chunk, me],
                send_sem=ysend_sem.at[chunk], recv_sem=yrecv_sem.at[chunk],
                device_id=place, device_id_type=MESH,
            ).start()

        sweep(visit)
        yrecv[chunk, me] = ysend[chunk, me]

    def take(piece):
        arrived = recv.at[piece, others]
        pltpu.make_async_copy(arrived, arrived, recv_sem.at[piece]).wait()
        lax.fori_loop(0, 8, functools.partial(widen, piece), 0)

    @pl.loop(0, CHUNKS)
    def _(chunk):
        take(chunk)
        lax.fori_loop(0, CC // BATCH, functools.partial(transform_taps, chunk), 0)

    @pl.loop(0, CHUNKS)
    def _(chunk):
        take(CHUNKS + chunk)
        lax.fori_loop(0, CC // BATCH, functools.partial(convolve, chunk), 0)
        lax.fori_loop(0, 8, functools.partial(narrow, chunk), 0)
        give_back(chunk)

    def gate(chunk, block, carry):
        lanes = lanes_of(chunk, block)
        convolved = yrecv[chunk, pl.ds(block * 8, 8)].reshape(128, TOK).T.astype(F32)
        product = (k_buf[:, lanes].astype(F32) * v_buf[:, lanes].astype(F32)).astype(BF16).astype(F32)
        out_buf[:, lanes] = (q_buf[:, lanes].astype(F32) * (convolved + gain_buf[:, lanes] * product)).astype(BF16)
        return carry

    for chunk in range(CHUNKS):
        arrived = yrecv.at[chunk, others]
        pltpu.make_async_copy(arrived, arrived, yrecv_sem.at[chunk]).wait()
        lax.fori_loop(0, BLOCKS, functools.partial(gate, chunk), 0, unroll=UNROLL)
    for piece in range(2 * CHUNKS):
        left = send.at[piece, others]
        pltpu.make_async_copy(left, left, send_sem.at[piece]).wait()
    for chunk in range(CHUNKS):
        left = ysend.at[chunk, others]
        pltpu.make_async_copy(left, left, ysend_sem.at[chunk]).wait()


def shards(query_proj, key_proj, value_proj, filter_taps, skip_gain):
    whole = (TOK, 4096)
    held = [
        pltpu.with_memory_space_constraint(a, pltpu.HBM)
        for a in (query_proj, key_proj, value_proj, filter_taps, skip_gain.reshape(1, 4096), *map(jnp.asarray, tables()))
    ]
    return pl.pallas_call(
        kernel,
        out_shape=pltpu.VMEM(whole, BF16),
        in_specs=[pl.BlockSpec(memory_space=pltpu.HBM)] * len(held),
        out_specs=pl.BlockSpec(memory_space=pltpu.VMEM),
        scratch_shapes=[
            pltpu.VMEM(whole, BF16), pltpu.VMEM(whole, BF16), pltpu.VMEM(whole, BF16), pltpu.VMEM(whole, BF16),
            pltpu.VMEM((1, 4096), F32),
            pltpu.VMEM((256, 128), BF16), pltpu.VMEM((256, 256), BF16), pltpu.VMEM((256, 256), BF16),
            pltpu.VMEM((128, 256), BF16), pltpu.VMEM((2, 128, 128), F32),
            pltpu.VMEM((2 * CHUNKS, DEVS, CC, TOK), BF16), pltpu.VMEM((2 * CHUNKS, DEVS, CC, TOK), BF16),
            pltpu.VMEM((DEVS * CC + CC, TOK), F32), pltpu.VMEM((CHUNKS * CC * 128, 256), F32), pltpu.VMEM((DEVS * CC + CC, TOK), F32),
            pltpu.VMEM((CHUNKS, DEVS, CC, TOK), BF16), pltpu.VMEM((CHUNKS, DEVS, CC, TOK), BF16),
            pltpu.SemaphoreType.DMA((10,)),
            pltpu.SemaphoreType.DMA((2 * CHUNKS,)), pltpu.SemaphoreType.DMA((2 * CHUNKS,)),
            pltpu.SemaphoreType.DMA((CHUNKS,)), pltpu.SemaphoreType.DMA((CHUNKS,)),
        ],
        compiler_params=pltpu.CompilerParams(
            collective_id=0, has_side_effects=True, vmem_limit_bytes=48 << 20
        ),
        cost_estimate=pl.CostEstimate(flops=3 << 30, bytes_accessed=6 << 20, transcendentals=0),
        name="long_conv",
    )(*held)


def solution(mesh):
    split = P(("seq", "chan"), None)
    return jax.shard_map(
        shards, mesh=mesh, in_specs=(split, split, split, split, P()), out_specs=split, check_vma=False
    )
```

```python
import functools
import math

import jax
import jax.numpy as jnp
import numpy as np
from jax import lax
from jax.experimental import pallas as pl
from jax.experimental.pallas import tpu as pltpu
from jax.sharding import PartitionSpec as P

MESH = pl.DeviceIdType.MESH
DEVS = 128
TOK = 128
CHUNKS = 2
CC = 16
BATCH = 16
UNROLL = 4
BLOCKS = 16
F32 = jnp.float32
BF16 = jnp.bfloat16


def tables():
    idx = np.arange(128)
    coarse = 2.0 * math.pi * np.outer(idx + 0.5, idx) / 256.0
    twist = 2.0 * math.pi * np.outer(idx + 0.5, idx) / 32768.0
    inner = 2.0 * math.pi * (np.outer(idx, idx) % 128) / 128.0
    fwd_outer = np.concatenate([np.cos(coarse), -np.sin(coarse)], axis=0)
    cos_in, sin_in = np.cos(inner), np.sin(inner)
    fwd_inner = np.block([[cos_in, -sin_in], [sin_in, cos_in]])
    inv_inner = np.block([[cos_in, sin_in], [-sin_in, cos_in]])
    inv_outer = np.concatenate([np.cos(coarse.T), -np.sin(coarse.T)], axis=1) * (2.0 / 32768.0)
    twists = np.stack([np.cos(twist), -np.sin(twist)])
    return (
        fwd_outer.astype(jnp.bfloat16),
        fwd_inner.astype(jnp.bfloat16),
        inv_inner.astype(jnp.bfloat16),
        inv_outer.astype(jnp.bfloat16),
        twists.astype(np.float32),
    )


STEPS = (
    84, 85, 86, 116, 77, 52, 87, 76, 93, 117, 83, 53, 92, 82, 45, 54,
    74, 91, 20, 95, 60, 75, 55, 109, 119, 79, 61, 115, 90, 124, 80, 125,
    118, 94, 44, 78, 21, 81, 108, 69, 114, 50, 68, 51, 42, 122, 43, 111,
    123, 63, 106, 62, 59, 46, 107, 126, 58, 47, 127, 110, 12, 72, 22, 70,
    13, 73, 101, 112, 19, 67, 18, 71, 29, 88, 49, 36, 28, 89, 66, 23,
    48, 100, 113, 37, 15, 102, 121, 98, 27, 120, 30, 40, 39, 99, 104, 31,
    38, 105, 14, 103, 11, 41, 34, 17, 35, 56, 10, 5, 64, 57, 26, 16,
    4, 65, 97, 9, 7, 8, 96, 3, 6, 25, 32, 2, 24, 33, 1,
)


def sweep(visit):
    seq, chan = lax.axis_index("seq"), lax.axis_index("chan")
    sense = 1 + 2 * (seq % 2)
    x, y, z = ([lax.rem(at + far * sense, 4) for far in range(4)] for at in (chan // 4, seq // 2, chan % 4))
    cores = (seq % 2, 1 - seq % 2)
    for code in STEPS:
        seq_to = y[code // 8 % 4] * 2 + cores[code % 2]
        chan_to = x[code // 32] * 4 + z[code // 2 % 4]
        visit(seq_to * 16 + chan_to, (seq_to, chan_to))


def kernel(
    q_hbm, k_hbm, v_hbm, h_hbm, gain_hbm, fo_hbm, fi_hbm, ii_hbm, io_hbm, tw_hbm, out_buf,
    q_buf, k_buf, v_buf, h_buf, gain_buf, fo_buf, fi_buf, ii_buf, io_buf, tw_buf,
    send, recv, wide, tap_spec, ywide, ysend, yrecv,
    in_sem, send_sem, recv_sem, ysend_sem, yrecv_sem,
):
    seq, chan = lax.axis_index("seq"), lax.axis_index("chan")
    me = seq * 16 + chan

    pairs = (
        (h_hbm, h_buf), (k_hbm, k_buf), (v_hbm, v_buf), (fo_hbm, fo_buf), (fi_hbm, fi_buf), (ii_hbm, ii_buf),
        (io_hbm, io_buf), (tw_hbm, tw_buf), (q_hbm, q_buf), (gain_hbm, gain_buf),
    )
    loads = [pltpu.make_async_copy(src, dst, in_sem.at[i]) for i, (src, dst) in enumerate(pairs)]

    def load_parts(i):
        for part in range(4):
            rows = pl.ds(part * (TOK // 4), TOK // 4)
            pltpu.make_async_copy(pairs[i][0].at[rows], pairs[i][1].at[rows], in_sem.at[i]).start()

    load_parts(0)
    barrier = pltpu.get_barrier_semaphore()
    sweep(lambda peer, place: pl.semaphore_signal(barrier, inc=1, device_id=place, device_id_type=MESH))
    for i in (1, 2):
        load_parts(i)
    for load in loads[3:]:
        load.start()

    def lanes_of(chunk, block):
        return pl.ds(pl.multiple_of(chunk * (BLOCKS * 128) + block * 128, 128), 128)

    def pack_taps(chunk, block, carry):
        send[chunk, pl.ds(block * 8, 8)] = h_buf[:, lanes_of(chunk, block)].T.reshape(8, CC, TOK)
        return carry

    def pack_product(chunk, block, carry):
        lanes = lanes_of(chunk, block)
        product = (k_buf[:, lanes].astype(F32) * v_buf[:, lanes].astype(F32)).astype(BF16)
        send[CHUNKS + chunk, pl.ds(block * 8, 8)] = product.T.reshape(8, CC, TOK)
        return carry

    def give(piece):
        def visit(peer, place):
            pltpu.make_async_remote_copy(
                src_ref=send.at[piece, peer], dst_ref=recv.at[piece, me],
                send_sem=send_sem.at[piece], recv_sem=recv_sem.at[piece],
                device_id=place, device_id_type=MESH,
            ).start()

        sweep(visit)

    def pack(body):
        lax.fori_loop(0, BLOCKS, body, 0, unroll=UNROLL)

    loads[0].wait()
    pack(functools.partial(pack_taps, 0))
    pl.semaphore_wait(barrier, DEVS - 1)

    @pl.loop(0, 2 * CHUNKS)
    def _(piece):
        @pl.when(piece == 1)
        def _():
            pack(functools.partial(pack_taps, 1))

        @pl.when(piece == CHUNKS)
        def _():
            loads[1].wait()
            loads[2].wait()

        @pl.when(piece >= CHUNKS)
        def _():
            pack(functools.partial(pack_product, piece - CHUNKS))

        give(piece)

    for piece in range(2 * CHUNKS):
        recv[piece, me] = send[piece, me]
    for load in loads[3:]:
        load.wait()

    others = pl.ds(0, DEVS - 1)

    def widen(piece, step, carry):
        rows = pl.ds(pl.multiple_of(step * (16 * CC), 16 * CC), 16 * CC)
        wide[rows, :] = recv[piece, pl.ds(step * 16, 16)].reshape(16 * CC, TOK).astype(F32)
        return carry

    def spectra(first):
        twist_re, twist_im = tw_buf[0], tw_buf[1]
        rows = []
        for c in range(0, BATCH, 2):
            both = jnp.concatenate(
                [wide[pl.ds(first + c + odd, DEVS, CC), :].astype(BF16) for odd in range(2)], axis=1)
            both = jnp.dot(fo_buf[...], both, preferred_element_type=F32)
            for lane in (0, 128):
                re, im = both[:128, lane:lane + 128], both[128:, lane:lane + 128]
                rows.append(jnp.concatenate(
                    [(re * twist_re - im * twist_im).astype(BF16), (re * twist_im + im * twist_re).astype(BF16)], axis=1))
        return jnp.dot(jnp.concatenate(rows, axis=0), fi_buf[...], preferred_element_type=F32)

    def transform_taps(chunk, at, carry):
        rows = pl.ds(pl.multiple_of((chunk * CC + at * BATCH) * 128, 128), BATCH * 128)
        tap_spec[rows, :] = spectra(at * BATCH)
        return carry

    def convolve(chunk, at, carry):
        twist_re, twist_im = tw_buf[0], tw_buf[1]
        x_all = spectra(at * BATCH)
        products = []
        for c in range(BATCH):
            taps = tap_spec[pl.ds(pl.multiple_of((chunk * CC + at * BATCH + c) * 128, 128), 128), :]
            x_re, x_im = x_all[c * 128:c * 128 + 128, :128], x_all[c * 128:c * 128 + 128, 128:]
            h_re, h_im = taps[:, :128], taps[:, 128:]
            products.append(jnp.concatenate(
                [(x_re * h_re - x_im * h_im).astype(BF16), (x_re * h_im + x_im * h_re).astype(BF16)], axis=1))
        back = jnp.dot(jnp.concatenate(products, axis=0), ii_buf[...], preferred_element_type=F32)
        turned = []
        for c in range(BATCH):
            re, im = back[c * 128:c * 128 + 128, :128], back[c * 128:c * 128 + 128, 128:]
            turned.append(jnp.concatenate(
                [(re * twist_re + im * twist_im).astype(BF16), (im * twist_re - re * twist_im).astype(BF16)], axis=0))
        for c in range(0, BATCH, 2):
            y = jnp.dot(io_buf[...], jnp.concatenate(turned[c:c + 2], axis=1), preferred_element_type=F32)
            ywide[pl.ds(BATCH * at + c, DEVS, CC), :] = y[:, :128]
            ywide[pl.ds(BATCH * at + c + 1, DEVS, CC), :] = y[:, 128:]
        return carry

    def narrow(chunk, step, carry):
        rows = pl.ds(pl.multiple_of(step * (16 * CC), 16 * CC), 16 * CC)
        ysend[chunk, pl.ds(step * 16, 16)] = ywide[rows, :].astype(BF16).reshape(16, CC, TOK)
        return carry

    def give_back(chunk):
        def visit(peer, place):
            pltpu.make_async_remote_copy(
                src_ref=ysend.at[chunk, peer], dst_ref=yrecv.at[chunk, me],
                send_sem=ysend_sem.at[chunk], recv_sem=yrecv_sem.at[chunk, me // 32],
                device_id=place, device_id_type=MESH,
            ).start()

        sweep(visit)
        pltpu.make_async_copy(ysend.at[chunk, me], yrecv.at[chunk, me], yrecv_sem.at[chunk, me // 32]).start()

    def take(piece):
        arrived = recv.at[piece, others]
        pltpu.make_async_copy(arrived, arrived, recv_sem.at[piece]).wait()
        lax.fori_loop(0, 8, functools.partial(widen, piece), 0)

    @pl.loop(0, CHUNKS)
    def _(chunk):
        take(chunk)
        lax.fori_loop(0, CC // BATCH, functools.partial(transform_taps, chunk), 0)

    @pl.loop(0, CHUNKS)
    def _(chunk):
        take(CHUNKS + chunk)
        lax.fori_loop(0, CC // BATCH, functools.partial(convolve, chunk), 0)
        lax.fori_loop(0, 8, functools.partial(narrow, chunk), 0)
        give_back(chunk)

    def gate(chunk, block, carry):
        lanes = lanes_of(chunk, block)
        convolved = yrecv[chunk, pl.ds(block * 8, 8)].reshape(128, TOK).T.astype(F32)
        product = (k_buf[:, lanes].astype(F32) * v_buf[:, lanes].astype(F32)).astype(BF16).astype(F32)
        out_buf[:, lanes] = (q_buf[:, lanes].astype(F32) * (convolved + gain_buf[:, lanes] * product)).astype(BF16)
        return carry

    for chunk in range(CHUNKS):
        for ahead in (2, 1, 3, 0):
            quarter = lax.rem(me // 32 + ahead, 4)
            arrived = yrecv.at[chunk, pl.ds(quarter * 32, 32)]
            pltpu.make_async_copy(arrived, arrived, yrecv_sem.at[chunk, quarter]).wait()
            for block in range(4):
                gate(chunk, quarter * 4 + block, 0)
    for piece in range(2 * CHUNKS):
        left = send.at[piece, others]
        pltpu.make_async_copy(left, left, send_sem.at[piece]).wait()
    for chunk in range(CHUNKS):
        left = ysend.at[chunk, others]
        pltpu.make_async_copy(left, left, ysend_sem.at[chunk]).wait()


def shards(query_proj, key_proj, value_proj, filter_taps, skip_gain):
    whole = (TOK, 4096)
    held = [
        pltpu.with_memory_space_constraint(a, pltpu.HBM)
        for a in (query_proj, key_proj, value_proj, filter_taps, skip_gain.reshape(1, 4096), *map(jnp.asarray, tables()))
    ]
    return pl.pallas_call(
        kernel,
        out_shape=pltpu.VMEM(whole, BF16),
        in_specs=[pl.BlockSpec(memory_space=pltpu.HBM)] * len(held),
        out_specs=pl.BlockSpec(memory_space=pltpu.VMEM),
        scratch_shapes=[
            pltpu.VMEM(whole, BF16), pltpu.VMEM(whole, BF16), pltpu.VMEM(whole, BF16), pltpu.VMEM(whole, BF16),
            pltpu.VMEM((1, 4096), F32),
            pltpu.VMEM((256, 128), BF16), pltpu.VMEM((256, 256), BF16), pltpu.VMEM((256, 256), BF16),
            pltpu.VMEM((128, 256), BF16), pltpu.VMEM((2, 128, 128), F32),
            pltpu.VMEM((2 * CHUNKS, DEVS, CC, TOK), BF16), pltpu.VMEM((2 * CHUNKS, DEVS, CC, TOK), BF16),
            pltpu.VMEM((DEVS * CC + CC, TOK), F32), pltpu.VMEM((CHUNKS * CC * 128, 256), F32), pltpu.VMEM((DEVS * CC + CC, TOK), F32),
            pltpu.VMEM((CHUNKS, DEVS, CC, TOK), BF16), pltpu.VMEM((CHUNKS, DEVS, CC, TOK), BF16),
            pltpu.SemaphoreType.DMA((10,)),
            pltpu.SemaphoreType.DMA((2 * CHUNKS,)), pltpu.SemaphoreType.DMA((2 * CHUNKS,)),
            pltpu.SemaphoreType.DMA((CHUNKS,)), pltpu.SemaphoreType.DMA((CHUNKS, 4)),
        ],
        compiler_params=pltpu.CompilerParams(
            collective_id=0, has_side_effects=True, vmem_limit_bytes=48 << 20
        ),
        cost_estimate=pl.CostEstimate(flops=3 << 30, bytes_accessed=6 << 20, transcendentals=0),
        name="long_conv",
    )(*held)


def solution(mesh):
    split = P(("seq", "chan"), None)
    return jax.shard_map(
        shards, mesh=mesh, in_specs=(split, split, split, split, P()), out_specs=split, check_vma=False
    )
```

```python
import functools
import math

import jax
import jax.numpy as jnp
import numpy as np
from jax import lax
from jax.experimental import pallas as pl
from jax.experimental.pallas import tpu as pltpu
from jax.sharding import PartitionSpec as P

MESH = pl.DeviceIdType.MESH
DEVS = 128
TOK = 128
CHUNKS = 2
CC = 16
BATCH = 16
UNROLL = 4
BLOCKS = 16
F32 = jnp.float32
BF16 = jnp.bfloat16


def tables():
    idx = np.arange(128)
    coarse = 2.0 * math.pi * np.outer(idx + 0.5, idx) / 256.0
    twist = 2.0 * math.pi * np.outer(idx + 0.5, idx) / 32768.0
    inner = 2.0 * math.pi * (np.outer(idx, idx) % 128) / 128.0
    fwd_outer = np.concatenate([np.cos(coarse), -np.sin(coarse)], axis=0)
    cos_in, sin_in = np.cos(inner), np.sin(inner)
    fwd_inner = np.block([[cos_in, -sin_in], [sin_in, cos_in]])
    inv_inner = np.block([[cos_in, sin_in], [-sin_in, cos_in]])
    inv_outer = np.concatenate([np.cos(coarse.T), -np.sin(coarse.T)], axis=1) * (2.0 / 32768.0)
    twists = np.stack([np.cos(twist), -np.sin(twist)])
    return (
        fwd_outer.astype(jnp.bfloat16),
        fwd_inner.astype(jnp.bfloat16),
        inv_inner.astype(jnp.bfloat16),
        inv_outer.astype(jnp.bfloat16),
        twists.astype(np.float32),
    )


STEPS = (
    84, 85, 86, 116, 77, 52, 87, 76, 93, 117, 83, 53, 92, 82, 45, 54,
    74, 91, 20, 95, 60, 75, 55, 109, 119, 79, 61, 115, 90, 124, 80, 125,
    118, 94, 44, 78, 21, 81, 108, 69, 114, 50, 68, 51, 42, 122, 43, 111,
    123, 63, 106, 62, 59, 46, 107, 126, 58, 47, 127, 110, 12, 72, 22, 70,
    13, 73, 101, 112, 19, 67, 18, 71, 29, 88, 49, 36, 28, 89, 66, 23,
    48, 100, 113, 37, 15, 102, 121, 98, 27, 120, 30, 40, 39, 99, 104, 31,
    38, 105, 14, 103, 11, 41, 34, 17, 35, 56, 10, 5, 64, 57, 26, 16,
    4, 65, 97, 9, 7, 8, 96, 3, 6, 25, 32, 2, 24, 33, 1,
)


def sweep(visit):
    seq, chan = lax.axis_index("seq"), lax.axis_index("chan")
    sense = 1 + 2 * (seq % 2)
    x, y, z = ([lax.rem(at + far * sense, 4) for far in range(4)] for at in (chan // 4, seq // 2, chan % 4))
    cores = (seq % 2, 1 - seq % 2)
    for code in STEPS:
        seq_to = y[code // 8 % 4] * 2 + cores[code % 2]
        chan_to = x[code // 32] * 4 + z[code // 2 % 4]
        visit(seq_to * 16 + chan_to, (seq_to, chan_to))


def kernel(
    q_hbm, k_hbm, v_hbm, h_hbm, gain_hbm, fo_hbm, fi_hbm, ii_hbm, io_hbm, tw_hbm, out_buf,
    q_buf, k_buf, v_buf, h_buf, gain_buf, fo_buf, fi_buf, ii_buf, io_buf, tw_buf,
    send, recv, wide, tap_spec, ywide, ysend, yrecv,
    in_sem, send_sem, recv_sem, ysend_sem, yrecv_sem,
):
    seq, chan = lax.axis_index("seq"), lax.axis_index("chan")
    me = seq * 16 + chan

    pairs = (
        (h_hbm, h_buf), (k_hbm, k_buf), (v_hbm, v_buf), (fo_hbm, fo_buf), (fi_hbm, fi_buf), (ii_hbm, ii_buf),
        (io_hbm, io_buf), (tw_hbm, tw_buf), (q_hbm, q_buf), (gain_hbm, gain_buf),
    )
    loads = [pltpu.make_async_copy(src, dst, in_sem.at[i]) for i, (src, dst) in enumerate(pairs)]

    def load_parts(i):
        for part in range(4):
            rows = pl.ds(part * (TOK // 4), TOK // 4)
            pltpu.make_async_copy(pairs[i][0].at[rows], pairs[i][1].at[rows], in_sem.at[i]).start()

    barrier = pltpu.get_barrier_semaphore()
    sweep(lambda peer, place: pl.semaphore_signal(barrier, inc=1, device_id=place, device_id_type=MESH))
    for i in range(3):
        load_parts(i)
    for load in loads[3:]:
        load.start()

    def lanes_of(chunk, block):
        return pl.ds(pl.multiple_of(chunk * (BLOCKS * 128) + block * 128, 128), 128)

    def pack_taps(chunk, block, carry):
        send[chunk, pl.ds(block * 8, 8)] = h_buf[:, lanes_of(chunk, block)].T.reshape(8, CC, TOK)
        return carry

    def pack_product(chunk, block, carry):
        lanes = lanes_of(chunk, block)
        product = (k_buf[:, lanes].astype(F32) * v_buf[:, lanes].astype(F32)).astype(BF16)
        send[CHUNKS + chunk, pl.ds(block * 8, 8)] = product.T.reshape(8, CC, TOK)
        return carry

    def give(piece):
        def visit(peer, place):
            pltpu.make_async_remote_copy(
                src_ref=send.at[piece, peer], dst_ref=recv.at[piece, me],
                send_sem=send_sem.at[piece], recv_sem=recv_sem.at[piece],
                device_id=place, device_id_type=MESH,
            ).start()

        sweep(visit)

    def pack(body):
        lax.fori_loop(0, BLOCKS, body, 0, unroll=UNROLL)

    loads[0].wait()
    pack(functools.partial(pack_taps, 0))
    pl.semaphore_wait(barrier, DEVS - 1)

    @pl.loop(0, 2 * CHUNKS)
    def _(piece):
        @pl.when(piece == 1)
        def _():
            pack(functools.partial(pack_taps, 1))

        @pl.when(piece == CHUNKS)
        def _():
            loads[1].wait()
            loads[2].wait()

        @pl.when(piece >= CHUNKS)
        def _():
            pack(functools.partial(pack_product, piece - CHUNKS))

        give(piece)

    for piece in range(2 * CHUNKS):
        recv[piece, me] = send[piece, me]
    for load in loads[3:]:
        load.wait()

    others = pl.ds(0, DEVS - 1)

    def widen(piece, step, carry):
        rows = pl.ds(pl.multiple_of(step * (16 * CC), 16 * CC), 16 * CC)
        wide[rows, :] = recv[piece, pl.ds(step * 16, 16)].reshape(16 * CC, TOK).astype(F32)
        return carry

    def spectra(first):
        twist_re, twist_im = tw_buf[0], tw_buf[1]
        rows = []
        for c in range(0, BATCH, 2):
            both = jnp.concatenate(
                [wide[pl.ds(first + c + odd, DEVS, CC), :].astype(BF16) for odd in range(2)], axis=1)
            both = jnp.dot(fo_buf[...], both, preferred_element_type=F32)
            for lane in (0, 128):
                re, im = both[:128, lane:lane + 128], both[128:, lane:lane + 128]
                rows.append(jnp.concatenate(
                    [(re * twist_re - im * twist_im).astype(BF16), (re * twist_im + im * twist_re).astype(BF16)], axis=1))
        return jnp.dot(jnp.concatenate(rows, axis=0), fi_buf[...], preferred_element_type=F32)

    def transform_taps(chunk, at, carry):
        rows = pl.ds(pl.multiple_of((chunk * CC + at * BATCH) * 128, 128), BATCH * 128)
        tap_spec[rows, :] = spectra(at * BATCH)
        return carry

    def convolve(chunk, at, carry):
        twist_re, twist_im = tw_buf[0], tw_buf[1]
        x_all = spectra(at * BATCH)
        products = []
        for c in range(BATCH):
            taps = tap_spec[pl.ds(pl.multiple_of((chunk * CC + at * BATCH + c) * 128, 128), 128), :]
            x_re, x_im = x_all[c * 128:c * 128 + 128, :128], x_all[c * 128:c * 128 + 128, 128:]
            h_re, h_im = taps[:, :128], taps[:, 128:]
            products.append(jnp.concatenate(
                [(x_re * h_re - x_im * h_im).astype(BF16), (x_re * h_im + x_im * h_re).astype(BF16)], axis=1))
        back = jnp.dot(jnp.concatenate(products, axis=0), ii_buf[...], preferred_element_type=F32)
        turned = []
        for c in range(BATCH):
            re, im = back[c * 128:c * 128 + 128, :128], back[c * 128:c * 128 + 128, 128:]
            turned.append(jnp.concatenate(
                [(re * twist_re + im * twist_im).astype(BF16), (im * twist_re - re * twist_im).astype(BF16)], axis=0))
        for c in range(0, BATCH, 2):
            y = jnp.dot(io_buf[...], jnp.concatenate(turned[c:c + 2], axis=1), preferred_element_type=F32)
            ywide[pl.ds(BATCH * at + c, DEVS, CC), :] = y[:, :128]
            ywide[pl.ds(BATCH * at + c + 1, DEVS, CC), :] = y[:, 128:]
        return carry

    def narrow(chunk, step, carry):
        rows = pl.ds(pl.multiple_of(step * (16 * CC), 16 * CC), 16 * CC)
        ysend[chunk, pl.ds(step * 16, 16)] = ywide[rows, :].astype(BF16).reshape(16, CC, TOK)
        return carry

    def give_back(chunk):
        def visit(peer, place):
            pltpu.make_async_remote_copy(
                src_ref=ysend.at[chunk, peer], dst_ref=yrecv.at[chunk, me],
                send_sem=ysend_sem.at[chunk], recv_sem=yrecv_sem.at[chunk, me // 32],
                device_id=place, device_id_type=MESH,
            ).start()

        sweep(visit)
        pltpu.make_async_copy(ysend.at[chunk, me], yrecv.at[chunk, me], yrecv_sem.at[chunk, me // 32]).start()

    def take(piece):
        arrived = recv.at[piece, others]
        pltpu.make_async_copy(arrived, arrived, recv_sem.at[piece]).wait()
        lax.fori_loop(0, 8, functools.partial(widen, piece), 0)

    @pl.loop(0, CHUNKS)
    def _(chunk):
        take(chunk)
        lax.fori_loop(0, CC // BATCH, functools.partial(transform_taps, chunk), 0)

    @pl.loop(0, CHUNKS)
    def _(chunk):
        take(CHUNKS + chunk)
        lax.fori_loop(0, CC // BATCH, functools.partial(convolve, chunk), 0)
        lax.fori_loop(0, 8, functools.partial(narrow, chunk), 0)
        give_back(chunk)

    def gate(chunk, block, carry):
        lanes = lanes_of(chunk, block)
        convolved = yrecv[chunk, pl.ds(block * 8, 8)].reshape(128, TOK).T.astype(F32)
        product = (k_buf[:, lanes].astype(F32) * v_buf[:, lanes].astype(F32)).astype(BF16).astype(F32)
        out_buf[:, lanes] = (q_buf[:, lanes].astype(F32) * (convolved + gain_buf[:, lanes] * product)).astype(BF16)
        return carry

    for chunk in range(CHUNKS):
        for ahead in (2, 1, 3, 0):
            quarter = lax.rem(me // 32 + ahead, 4)
            arrived = yrecv.at[chunk, pl.ds(quarter * 32, 32)]
            pltpu.make_async_copy(arrived, arrived, yrecv_sem.at[chunk, quarter]).wait()
            for block in range(4):
                gate(chunk, quarter * 4 + block, 0)
    for piece in range(2 * CHUNKS):
        left = send.at[piece, others]
        pltpu.make_async_copy(left, left, send_sem.at[piece]).wait()
    for chunk in range(CHUNKS):
        left = ysend.at[chunk, others]
        pltpu.make_async_copy(left, left, ysend_sem.at[chunk]).wait()


def shards(query_proj, key_proj, value_proj, filter_taps, skip_gain):
    whole = (TOK, 4096)
    held = [
        pltpu.with_memory_space_constraint(a, pltpu.HBM)
        for a in (query_proj, key_proj, value_proj, filter_taps, skip_gain.reshape(1, 4096), *map(jnp.asarray, tables()))
    ]
    return pl.pallas_call(
        kernel,
        out_shape=pltpu.VMEM(whole, BF16),
        in_specs=[pl.BlockSpec(memory_space=pltpu.HBM)] * len(held),
        out_specs=pl.BlockSpec(memory_space=pltpu.VMEM),
        scratch_shapes=[
            pltpu.VMEM(whole, BF16), pltpu.VMEM(whole, BF16), pltpu.VMEM(whole, BF16), pltpu.VMEM(whole, BF16),
            pltpu.VMEM((1, 4096), F32),
            pltpu.VMEM((256, 128), BF16), pltpu.VMEM((256, 256), BF16), pltpu.VMEM((256, 256), BF16),
            pltpu.VMEM((128, 256), BF16), pltpu.VMEM((2, 128, 128), F32),
            pltpu.VMEM((2 * CHUNKS, DEVS, CC, TOK), BF16), pltpu.VMEM((2 * CHUNKS, DEVS, CC, TOK), BF16),
            pltpu.VMEM((DEVS * CC + CC, TOK), F32), pltpu.VMEM((CHUNKS * CC * 128, 256), F32), pltpu.VMEM((DEVS * CC + CC, TOK), F32),
            pltpu.VMEM((CHUNKS, DEVS, CC, TOK), BF16), pltpu.VMEM((CHUNKS, DEVS, CC, TOK), BF16),
            pltpu.SemaphoreType.DMA((10,)),
            pltpu.SemaphoreType.DMA((2 * CHUNKS,)), pltpu.SemaphoreType.DMA((2 * CHUNKS,)),
            pltpu.SemaphoreType.DMA((CHUNKS,)), pltpu.SemaphoreType.DMA((CHUNKS, 4)),
        ],
        compiler_params=pltpu.CompilerParams(
            collective_id=0, has_side_effects=True, vmem_limit_bytes=48 << 20
        ),
        cost_estimate=pl.CostEstimate(flops=3 << 30, bytes_accessed=6 << 20, transcendentals=0),
        name="long_conv",
    )(*held)


def solution(mesh):
    split = P(("seq", "chan"), None)
    return jax.shard_map(
        shards, mesh=mesh, in_specs=(split, split, split, split, P()), out_specs=split, check_vma=False
    )
```

```python
import functools
import math

import jax
import jax.numpy as jnp
import numpy as np
from jax import lax
from jax.experimental import pallas as pl
from jax.experimental.pallas import tpu as pltpu
from jax.sharding import PartitionSpec as P

MESH = pl.DeviceIdType.MESH
DEVS = 128
TOK = 128
CHUNKS = 2
CC = 16
BATCH = 16
UNROLL = 4
BLOCKS = 16
F32 = jnp.float32
BF16 = jnp.bfloat16


def tables():
    idx = np.arange(128)
    coarse = 2.0 * math.pi * np.outer(idx + 0.5, idx) / 256.0
    twist = 2.0 * math.pi * np.outer(idx + 0.5, idx) / 32768.0
    inner = 2.0 * math.pi * (np.outer(idx, idx) % 128) / 128.0
    fwd_outer = np.concatenate([np.cos(coarse), -np.sin(coarse)], axis=0)
    cos_in, sin_in = np.cos(inner), np.sin(inner)
    fwd_inner = np.block([[cos_in, -sin_in], [sin_in, cos_in]])
    inv_inner = np.block([[cos_in, sin_in], [-sin_in, cos_in]])
    inv_outer = np.concatenate([np.cos(coarse.T), -np.sin(coarse.T)], axis=1) * (2.0 / 32768.0)
    twists = np.stack([np.cos(twist), -np.sin(twist)])
    return (
        fwd_outer.astype(jnp.bfloat16),
        fwd_inner.astype(jnp.bfloat16),
        inv_inner.astype(jnp.bfloat16),
        inv_outer.astype(jnp.bfloat16),
        twists.astype(np.float32),
    )


STEPS = (
    84, 85, 86, 116, 77, 52, 87, 76, 93, 117, 83, 53, 92, 82, 45, 54,
    74, 91, 20, 95, 60, 75, 55, 109, 119, 79, 61, 115, 90, 124, 80, 125,
    118, 94, 44, 78, 21, 81, 108, 69, 114, 50, 68, 51, 42, 122, 43, 111,
    123, 63, 106, 62, 59, 46, 107, 126, 58, 47, 127, 110, 12, 72, 22, 70,
    13, 73, 101, 112, 19, 67, 18, 71, 29, 88, 49, 36, 28, 89, 66, 23,
    48, 100, 113, 37, 15, 102, 121, 98, 27, 120, 30, 40, 39, 99, 104, 31,
    38, 105, 14, 103, 11, 41, 34, 17, 35, 56, 10, 5, 64, 57, 26, 16,
    4, 65, 97, 9, 7, 8, 96, 3, 6, 25, 32, 2, 24, 33, 1,
)


def sweep(visit):
    seq, chan = lax.axis_index("seq"), lax.axis_index("chan")
    sense = 1 + 2 * (seq % 2)
    x, y, z = ([lax.rem(at + far * sense, 4) for far in range(4)] for at in (chan // 4, seq // 2, chan % 4))
    cores = (seq % 2, 1 - seq % 2)
    for code in STEPS:
        seq_to = y[code // 8 % 4] * 2 + cores[code % 2]
        chan_to = x[code // 32] * 4 + z[code // 2 % 4]
        visit(seq_to * 16 + chan_to, (seq_to, chan_to))


def kernel(
    q_hbm, k_hbm, v_hbm, h_hbm, gain_hbm, fo_hbm, fi_hbm, ii_hbm, io_hbm, tw_hbm, out_buf,
    q_buf, k_buf, v_buf, h_buf, gain_buf, fo_buf, fi_buf, ii_buf, io_buf, tw_buf,
    send, recv, wide, tap_spec, ywide, ysend, yrecv,
    in_sem, send_sem, recv_sem, ysend_sem, yrecv_sem,
):
    seq, chan = lax.axis_index("seq"), lax.axis_index("chan")
    me = seq * 16 + chan

    pairs = (
        (h_hbm, h_buf), (k_hbm, k_buf), (v_hbm, v_buf), (fo_hbm, fo_buf), (fi_hbm, fi_buf), (ii_hbm, ii_buf),
        (io_hbm, io_buf), (tw_hbm, tw_buf), (q_hbm, q_buf), (gain_hbm, gain_buf),
    )
    loads = [pltpu.make_async_copy(src, dst, in_sem.at[i]) for i, (src, dst) in enumerate(pairs)]

    barrier = pltpu.get_barrier_semaphore()
    sweep(lambda peer, place: pl.semaphore_signal(barrier, inc=1, device_id=place, device_id_type=MESH))
    for load in loads:
        load.start()

    def lanes_of(chunk, block):
        return pl.ds(pl.multiple_of(chunk * (BLOCKS * 128) + block * 128, 128), 128)

    def pack_taps(chunk, block, carry):
        send[chunk, pl.ds(block * 8, 8)] = h_buf[:, lanes_of(chunk, block)].T.reshape(8, CC, TOK)
        return carry

    def pack_product(chunk, block, carry):
        lanes = lanes_of(chunk, block)
        product = (k_buf[:, lanes].astype(F32) * v_buf[:, lanes].astype(F32)).astype(BF16)
        send[CHUNKS + chunk, pl.ds(block * 8, 8)] = product.T.reshape(8, CC, TOK)
        return carry

    def give(piece):
        def visit(peer, place):
            pltpu.make_async_remote_copy(
                src_ref=send.at[piece, peer], dst_ref=recv.at[piece, me],
                send_sem=send_sem.at[piece], recv_sem=recv_sem.at[piece],
                device_id=place, device_id_type=MESH,
            ).start()

        sweep(visit)

    def pack(body):
        lax.fori_loop(0, BLOCKS, body, 0, unroll=UNROLL)

    loads[0].wait()
    pack(functools.partial(pack_taps, 0))
    pl.semaphore_wait(barrier, DEVS - 1)

    @pl.loop(0, 2 * CHUNKS)
    def _(piece):
        @pl.when(piece == 1)
        def _():
            pack(functools.partial(pack_taps, 1))

        @pl.when(piece == CHUNKS)
        def _():
            loads[1].wait()
            loads[2].wait()

        @pl.when(piece >= CHUNKS)
        def _():
            pack(functools.partial(pack_product, piece - CHUNKS))

        give(piece)

    for piece in range(2 * CHUNKS):
        recv[piece, me] = send[piece, me]
    for load in loads[3:]:
        load.wait()

    others = pl.ds(0, DEVS - 1)

    def widen(piece, step, carry):
        rows = pl.ds(pl.multiple_of(step * (16 * CC), 16 * CC), 16 * CC)
        wide[rows, :] = recv[piece, pl.ds(step * 16, 16)].reshape(16 * CC, TOK).astype(F32)
        return carry

    def spectra(first):
        twist_re, twist_im = tw_buf[0], tw_buf[1]
        rows = []
        for c in range(0, BATCH, 2):
            both = jnp.concatenate(
                [wide[pl.ds(first + c + odd, DEVS, CC), :].astype(BF16) for odd in range(2)], axis=1)
            both = jnp.dot(fo_buf[...], both, preferred_element_type=F32)
            for lane in (0, 128):
                re, im = both[:128, lane:lane + 128], both[128:, lane:lane + 128]
                rows.append(jnp.concatenate(
                    [(re * twist_re - im * twist_im).astype(BF16), (re * twist_im + im * twist_re).astype(BF16)], axis=1))
        return jnp.dot(jnp.concatenate(rows, axis=0), fi_buf[...], preferred_element_type=F32)

    def transform_taps(chunk, at, carry):
        rows = pl.ds(pl.multiple_of((chunk * CC + at * BATCH) * 128, 128), BATCH * 128)
        tap_spec[rows, :] = spectra(at * BATCH)
        return carry

    def convolve(chunk, at, carry):
        twist_re, twist_im = tw_buf[0], tw_buf[1]
        x_all = spectra(at * BATCH)
        products = []
        for c in range(BATCH):
            taps = tap_spec[pl.ds(pl.multiple_of((chunk * CC + at * BATCH + c) * 128, 128), 128), :]
            x_re, x_im = x_all[c * 128:c * 128 + 128, :128], x_all[c * 128:c * 128 + 128, 128:]
            h_re, h_im = taps[:, :128], taps[:, 128:]
            products.append(jnp.concatenate(
                [(x_re * h_re - x_im * h_im).astype(BF16), (x_re * h_im + x_im * h_re).astype(BF16)], axis=1))
        back = jnp.dot(jnp.concatenate(products, axis=0), ii_buf[...], preferred_element_type=F32)
        turned = []
        for c in range(BATCH):
            re, im = back[c * 128:c * 128 + 128, :128], back[c * 128:c * 128 + 128, 128:]
            turned.append(jnp.concatenate(
                [(re * twist_re + im * twist_im).astype(BF16), (im * twist_re - re * twist_im).astype(BF16)], axis=0))
        for c in range(0, BATCH, 2):
            y = jnp.dot(io_buf[...], jnp.concatenate(turned[c:c + 2], axis=1), preferred_element_type=F32)
            ywide[pl.ds(BATCH * at + c, DEVS, CC), :] = y[:, :128]
            ywide[pl.ds(BATCH * at + c + 1, DEVS, CC), :] = y[:, 128:]
        return carry

    def narrow(chunk, step, carry):
        rows = pl.ds(pl.multiple_of(step * (16 * CC), 16 * CC), 16 * CC)
        ysend[chunk, pl.ds(step * 16, 16)] = ywide[rows, :].astype(BF16).reshape(16, CC, TOK)
        return carry

    def give_back(chunk):
        def visit(peer, place):
            pltpu.make_async_remote_copy(
                src_ref=ysend.at[chunk, peer], dst_ref=yrecv.at[chunk, me],
                send_sem=ysend_sem.at[chunk], recv_sem=yrecv_sem.at[chunk, me // 32],
                device_id=place, device_id_type=MESH,
            ).start()

        sweep(visit)
        pltpu.make_async_copy(ysend.at[chunk, me], yrecv.at[chunk, me], yrecv_sem.at[chunk, me // 32]).start()

    def take(piece):
        arrived = recv.at[piece, others]
        pltpu.make_async_copy(arrived, arrived, recv_sem.at[piece]).wait()
        lax.fori_loop(0, 8, functools.partial(widen, piece), 0, unroll=UNROLL)

    @pl.loop(0, CHUNKS)
    def _(chunk):
        take(chunk)
        lax.fori_loop(0, CC // BATCH, functools.partial(transform_taps, chunk), 0)

    @pl.loop(0, CHUNKS)
    def _(chunk):
        take(CHUNKS + chunk)
        lax.fori_loop(0, CC // BATCH, functools.partial(convolve, chunk), 0)
        lax.fori_loop(0, 8, functools.partial(narrow, chunk), 0, unroll=UNROLL)
        give_back(chunk)

    def gate(chunk, block, carry):
        lanes = lanes_of(chunk, block)
        convolved = yrecv[chunk, pl.ds(block * 8, 8)].reshape(128, TOK).T.astype(F32)
        product = (k_buf[:, lanes].astype(F32) * v_buf[:, lanes].astype(F32)).astype(BF16).astype(F32)
        out_buf[:, lanes] = (q_buf[:, lanes].astype(F32) * (convolved + gain_buf[:, lanes] * product)).astype(BF16)
        return carry

    for chunk in range(CHUNKS):
        for ahead in (2, 1, 3, 0):
            quarter = lax.rem(me // 32 + ahead, 4)
            arrived = yrecv.at[chunk, pl.ds(quarter * 32, 32)]
            pltpu.make_async_copy(arrived, arrived, yrecv_sem.at[chunk, quarter]).wait()
            for block in range(4):
                gate(chunk, quarter * 4 + block, 0)
    for piece in range(2 * CHUNKS):
        left = send.at[piece, others]
        pltpu.make_async_copy(left, left, send_sem.at[piece]).wait()
    for chunk in range(CHUNKS):
        left = ysend.at[chunk, others]
        pltpu.make_async_copy(left, left, ysend_sem.at[chunk]).wait()


def shards(query_proj, key_proj, value_proj, filter_taps, skip_gain):
    whole = (TOK, 4096)
    held = [
        pltpu.with_memory_space_constraint(a, pltpu.HBM)
        for a in (query_proj, key_proj, value_proj, filter_taps, skip_gain.reshape(1, 4096), *map(jnp.asarray, tables()))
    ]
    return pl.pallas_call(
        kernel,
        out_shape=pltpu.VMEM(whole, BF16),
        in_specs=[pl.BlockSpec(memory_space=pltpu.HBM)] * len(held),
        out_specs=pl.BlockSpec(memory_space=pltpu.VMEM),
        scratch_shapes=[
            pltpu.VMEM(whole, BF16), pltpu.VMEM(whole, BF16), pltpu.VMEM(whole, BF16), pltpu.VMEM(whole, BF16),
            pltpu.VMEM((1, 4096), F32),
            pltpu.VMEM((256, 128), BF16), pltpu.VMEM((256, 256), BF16), pltpu.VMEM((256, 256), BF16),
            pltpu.VMEM((128, 256), BF16), pltpu.VMEM((2, 128, 128), F32),
            pltpu.VMEM((2 * CHUNKS, DEVS, CC, TOK), BF16), pltpu.VMEM((2 * CHUNKS, DEVS, CC, TOK), BF16),
            pltpu.VMEM((DEVS * CC + CC, TOK), F32), pltpu.VMEM((CHUNKS * CC * 128, 256), F32), pltpu.VMEM((DEVS * CC + CC, TOK), F32),
            pltpu.VMEM((CHUNKS, DEVS, CC, TOK), BF16), pltpu.VMEM((CHUNKS, DEVS, CC, TOK), BF16),
            pltpu.SemaphoreType.DMA((10,)),
            pltpu.SemaphoreType.DMA((2 * CHUNKS,)), pltpu.SemaphoreType.DMA((2 * CHUNKS,)),
            pltpu.SemaphoreType.DMA((CHUNKS,)), pltpu.SemaphoreType.DMA((CHUNKS, 4)),
        ],
        compiler_params=pltpu.CompilerParams(
            collective_id=0, has_side_effects=True, vmem_limit_bytes=48 << 20
        ),
        cost_estimate=pl.CostEstimate(flops=3 << 30, bytes_accessed=6 << 20, transcendentals=0),
        name="long_conv",
    )(*held)


def solution(mesh):
    split = P(("seq", "chan"), None)
    return jax.shard_map(
        shards, mesh=mesh, in_specs=(split, split, split, split, P()), out_specs=split, check_vma=False
    )
```

```python
import functools
import math

import jax
import jax.numpy as jnp
import numpy as np
from jax import lax
from jax.experimental import pallas as pl
from jax.experimental.pallas import tpu as pltpu
from jax.sharding import PartitionSpec as P

MESH = pl.DeviceIdType.MESH
DEVS = 128
TOK = 128
CHUNKS = 2
CC = 16
BATCH = 16
UNROLL = 8
BLOCKS = 16
F32 = jnp.float32
BF16 = jnp.bfloat16


def tables():
    idx = np.arange(128)
    coarse = 2.0 * math.pi * np.outer(idx + 0.5, idx) / 256.0
    twist = 2.0 * math.pi * np.outer(idx + 0.5, idx) / 32768.0
    inner = 2.0 * math.pi * (np.outer(idx, idx) % 128) / 128.0
    fwd_outer = np.concatenate([np.cos(coarse), -np.sin(coarse)], axis=0)
    cos_in, sin_in = np.cos(inner), np.sin(inner)
    fwd_inner = np.block([[cos_in, -sin_in], [sin_in, cos_in]])
    inv_inner = np.block([[cos_in, sin_in], [-sin_in, cos_in]])
    inv_outer = np.concatenate([np.cos(coarse.T), -np.sin(coarse.T)], axis=1) * (2.0 / 32768.0)
    twists = np.stack([np.cos(twist), -np.sin(twist)])
    return (
        fwd_outer.astype(jnp.bfloat16),
        fwd_inner.astype(jnp.bfloat16),
        inv_inner.astype(jnp.bfloat16),
        inv_outer.astype(jnp.bfloat16),
        twists.astype(np.float32),
    )


STEPS = (
    84, 85, 86, 116, 77, 52, 87, 76, 93, 117, 83, 53, 92, 82, 45, 54,
    74, 91, 20, 95, 60, 75, 55, 109, 119, 79, 61, 115, 90, 124, 80, 125,
    118, 94, 44, 78, 21, 81, 108, 69, 114, 50, 68, 51, 42, 122, 43, 111,
    123, 63, 106, 62, 59, 46, 107, 126, 58, 47, 127, 110, 12, 72, 22, 70,
    13, 73, 101, 112, 19, 67, 18, 71, 29, 88, 49, 36, 28, 89, 66, 23,
    48, 100, 113, 37, 15, 102, 121, 98, 27, 120, 30, 40, 39, 99, 104, 31,
    38, 105, 14, 103, 11, 41, 34, 17, 35, 56, 10, 5, 64, 57, 26, 16,
    4, 65, 97, 9, 7, 8, 96, 3, 6, 25, 32, 2, 24, 33, 1,
)


def sweep(visit):
    seq, chan = lax.axis_index("seq"), lax.axis_index("chan")
    sense = 1 + 2 * (seq % 2)
    x, y, z = ([lax.rem(at + far * sense, 4) for far in range(4)] for at in (chan // 4, seq // 2, chan % 4))
    cores = (seq % 2, 1 - seq % 2)
    for code in STEPS:
        seq_to = y[code // 8 % 4] * 2 + cores[code % 2]
        chan_to = x[code // 32] * 4 + z[code // 2 % 4]
        visit(seq_to * 16 + chan_to, (seq_to, chan_to))


def kernel(
    q_hbm, k_hbm, v_hbm, h_hbm, gain_hbm, fo_hbm, fi_hbm, ii_hbm, io_hbm, tw_hbm, out_buf,
    q_buf, k_buf, v_buf, h_buf, gain_buf, fo_buf, fi_buf, ii_buf, io_buf, tw_buf,
    send, recv, wide, tap_spec, ywide, ysend, yrecv,
    in_sem, send_sem, recv_sem, ysend_sem, yrecv_sem,
):
    seq, chan = lax.axis_index("seq"), lax.axis_index("chan")
    me = seq * 16 + chan

    pairs = (
        (h_hbm, h_buf), (k_hbm, k_buf), (v_hbm, v_buf), (fo_hbm, fo_buf), (fi_hbm, fi_buf), (ii_hbm, ii_buf),
        (io_hbm, io_buf), (tw_hbm, tw_buf), (q_hbm, q_buf), (gain_hbm, gain_buf),
    )
    loads = [pltpu.make_async_copy(src, dst, in_sem.at[i]) for i, (src, dst) in enumerate(pairs)]

    barrier = pltpu.get_barrier_semaphore()
    sweep(lambda peer, place: pl.semaphore_signal(barrier, inc=1, device_id=place, device_id_type=MESH))
    for load in loads:
        load.start()

    def lanes_of(chunk, block):
        return pl.ds(pl.multiple_of(chunk * (BLOCKS * 128) + block * 128, 128), 128)

    def pack_taps(chunk, block, carry):
        send[chunk, pl.ds(block * 8, 8)] = h_buf[:, lanes_of(chunk, block)].T.reshape(8, CC, TOK)
        return carry

    def pack_product(chunk, block, carry):
        lanes = lanes_of(chunk, block)
        product = (k_buf[:, lanes].astype(F32) * v_buf[:, lanes].astype(F32)).astype(BF16)
        send[CHUNKS + chunk, pl.ds(block * 8, 8)] = product.T.reshape(8, CC, TOK)
        return carry

    def give(piece):
        def visit(peer, place):
            pltpu.make_async_remote_copy(
                src_ref=send.at[piece, peer], dst_ref=recv.at[piece, me],
                send_sem=send_sem.at[piece], recv_sem=recv_sem.at[piece],
                device_id=place, device_id_type=MESH,
            ).start()

        sweep(visit)

    def pack(body):
        lax.fori_loop(0, BLOCKS, body, 0, unroll=UNROLL)

    loads[0].wait()
    pack(functools.partial(pack_taps, 0))
    pl.semaphore_wait(barrier, DEVS - 1)

    @pl.loop(0, 2 * CHUNKS)
    def _(piece):
        @pl.when(piece == 1)
        def _():
            pack(functools.partial(pack_taps, 1))

        @pl.when(piece == CHUNKS)
        def _():
            loads[1].wait()
            loads[2].wait()

        @pl.when(piece >= CHUNKS)
        def _():
            pack(functools.partial(pack_product, piece - CHUNKS))

        give(piece)

    for piece in range(2 * CHUNKS):
        recv[piece, me] = send[piece, me]
    for load in loads[3:]:
        load.wait()

    others = pl.ds(0, DEVS - 1)

    def widen(piece, step, carry):
        rows = pl.ds(pl.multiple_of(step * (16 * CC), 16 * CC), 16 * CC)
        wide[rows, :] = recv[piece, pl.ds(step * 16, 16)].reshape(16 * CC, TOK).astype(F32)
        return carry

    def spectra(first):
        twist_re, twist_im = tw_buf[0], tw_buf[1]
        rows = []
        for c in range(0, BATCH, 2):
            both = jnp.concatenate(
                [wide[pl.ds(first + c + odd, DEVS, CC), :].astype(BF16) for odd in range(2)], axis=1)
            both = jnp.dot(fo_buf[...], both, preferred_element_type=F32)
            for lane in (0, 128):
                re, im = both[:128, lane:lane + 128], both[128:, lane:lane + 128]
                rows.append(jnp.concatenate(
                    [(re * twist_re - im * twist_im).astype(BF16), (re * twist_im + im * twist_re).astype(BF16)], axis=1))
        return jnp.dot(jnp.concatenate(rows, axis=0), fi_buf[...], preferred_element_type=F32)

    def transform_taps(chunk, at, carry):
        rows = pl.ds(pl.multiple_of((chunk * CC + at * BATCH) * 128, 128), BATCH * 128)
        tap_spec[rows, :] = spectra(at * BATCH)
        return carry

    def convolve(chunk, at, carry):
        twist_re, twist_im = tw_buf[0], tw_buf[1]
        x_all = spectra(at * BATCH)
        products = []
        for c in range(BATCH):
            taps = tap_spec[pl.ds(pl.multiple_of((chunk * CC + at * BATCH + c) * 128, 128), 128), :]
            x_re, x_im = x_all[c * 128:c * 128 + 128, :128], x_all[c * 128:c * 128 + 128, 128:]
            h_re, h_im = taps[:, :128], taps[:, 128:]
            products.append(jnp.concatenate(
                [(x_re * h_re - x_im * h_im).astype(BF16), (x_re * h_im + x_im * h_re).astype(BF16)], axis=1))
        back = jnp.dot(jnp.concatenate(products, axis=0), ii_buf[...], preferred_element_type=F32)
        turned = []
        for c in range(BATCH):
            re, im = back[c * 128:c * 128 + 128, :128], back[c * 128:c * 128 + 128, 128:]
            turned.append(jnp.concatenate(
                [(re * twist_re + im * twist_im).astype(BF16), (im * twist_re - re * twist_im).astype(BF16)], axis=0))
        for c in range(0, BATCH, 2):
            y = jnp.dot(io_buf[...], jnp.concatenate(turned[c:c + 2], axis=1), preferred_element_type=F32)
            ywide[pl.ds(BATCH * at + c, DEVS, CC), :] = y[:, :128]
            ywide[pl.ds(BATCH * at + c + 1, DEVS, CC), :] = y[:, 128:]
        return carry

    def narrow(chunk, step, carry):
        rows = pl.ds(pl.multiple_of(step * (16 * CC), 16 * CC), 16 * CC)
        ysend[chunk, pl.ds(step * 16, 16)] = ywide[rows, :].astype(BF16).reshape(16, CC, TOK)
        return carry

    def give_back(chunk):
        def visit(peer, place):
            pltpu.make_async_remote_copy(
                src_ref=ysend.at[chunk, peer], dst_ref=yrecv.at[chunk, me],
                send_sem=ysend_sem.at[chunk], recv_sem=yrecv_sem.at[chunk, me // 32],
                device_id=place, device_id_type=MESH,
            ).start()

        sweep(visit)
        pltpu.make_async_copy(ysend.at[chunk, me], yrecv.at[chunk, me], yrecv_sem.at[chunk, me // 32]).start()

    def take(piece):
        arrived = recv.at[piece, others]
        pltpu.make_async_copy(arrived, arrived, recv_sem.at[piece]).wait()
        lax.fori_loop(0, 8, functools.partial(widen, piece), 0, unroll=UNROLL)

    @pl.loop(0, CHUNKS)
    def _(chunk):
        take(chunk)
        lax.fori_loop(0, CC // BATCH, functools.partial(transform_taps, chunk), 0)

    @pl.loop(0, CHUNKS)
    def _(chunk):
        take(CHUNKS + chunk)
        lax.fori_loop(0, CC // BATCH, functools.partial(convolve, chunk), 0)
        lax.fori_loop(0, 8, functools.partial(narrow, chunk), 0, unroll=UNROLL)
        give_back(chunk)

    def gate(chunk, block, carry):
        lanes = lanes_of(chunk, block)
        convolved = yrecv[chunk, pl.ds(block * 8, 8)].reshape(128, TOK).T.astype(F32)
        product = (k_buf[:, lanes].astype(F32) * v_buf[:, lanes].astype(F32)).astype(BF16).astype(F32)
        out_buf[:, lanes] = (q_buf[:, lanes].astype(F32) * (convolved + gain_buf[:, lanes] * product)).astype(BF16)
        return carry

    for chunk in range(CHUNKS):
        for ahead in (2, 1, 3, 0):
            quarter = lax.rem(me // 32 + ahead, 4)
            arrived = yrecv.at[chunk, pl.ds(quarter * 32, 32)]
            pltpu.make_async_copy(arrived, arrived, yrecv_sem.at[chunk, quarter]).wait()
            for block in range(4):
                gate(chunk, quarter * 4 + block, 0)
    for piece in range(2 * CHUNKS):
        left = send.at[piece, others]
        pltpu.make_async_copy(left, left, send_sem.at[piece]).wait()
    for chunk in range(CHUNKS):
        left = ysend.at[chunk, others]
        pltpu.make_async_copy(left, left, ysend_sem.at[chunk]).wait()


def shards(query_proj, key_proj, value_proj, filter_taps, skip_gain):
    whole = (TOK, 4096)
    held = [
        pltpu.with_memory_space_constraint(a, pltpu.HBM)
        for a in (query_proj, key_proj, value_proj, filter_taps, skip_gain.reshape(1, 4096), *map(jnp.asarray, tables()))
    ]
    return pl.pallas_call(
        kernel,
        out_shape=pltpu.VMEM(whole, BF16),
        in_specs=[pl.BlockSpec(memory_space=pltpu.HBM)] * len(held),
        out_specs=pl.BlockSpec(memory_space=pltpu.VMEM),
        scratch_shapes=[
            pltpu.VMEM(whole, BF16), pltpu.VMEM(whole, BF16), pltpu.VMEM(whole, BF16), pltpu.VMEM(whole, BF16),
            pltpu.VMEM((1, 4096), F32),
            pltpu.VMEM((256, 128), BF16), pltpu.VMEM((256, 256), BF16), pltpu.VMEM((256, 256), BF16),
            pltpu.VMEM((128, 256), BF16), pltpu.VMEM((2, 128, 128), F32),
            pltpu.VMEM((2 * CHUNKS, DEVS, CC, TOK), BF16), pltpu.VMEM((2 * CHUNKS, DEVS, CC, TOK), BF16),
            pltpu.VMEM((DEVS * CC + CC, TOK), F32), pltpu.VMEM((CHUNKS * CC * 128, 256), F32), pltpu.VMEM((DEVS * CC + CC, TOK), F32),
            pltpu.VMEM((CHUNKS, DEVS, CC, TOK), BF16), pltpu.VMEM((CHUNKS, DEVS, CC, TOK), BF16),
            pltpu.SemaphoreType.DMA((10,)),
            pltpu.SemaphoreType.DMA((2 * CHUNKS,)), pltpu.SemaphoreType.DMA((2 * CHUNKS,)),
            pltpu.SemaphoreType.DMA((CHUNKS,)), pltpu.SemaphoreType.DMA((CHUNKS, 4)),
        ],
        compiler_params=pltpu.CompilerParams(
            collective_id=0, has_side_effects=True, vmem_limit_bytes=48 << 20
        ),
        cost_estimate=pl.CostEstimate(flops=3 << 30, bytes_accessed=6 << 20, transcendentals=0),
        name="long_conv",
    )(*held)


def solution(mesh):
    split = P(("seq", "chan"), None)
    return jax.shard_map(
        shards, mesh=mesh, in_specs=(split, split, split, split, P()), out_specs=split, check_vma=False
    )
```
